32 devices in a mesh: obj: 4 (over x, core), tile: 8 (over z, y).
Axes of the slice: x: 2, y: 2, z: 4, core: 2. Of those that a mesh axis runs over, the one named last changes fastest.
Arguments:
- checkpoints: bfloat16 [6, 12, 48, 8, 128], P(None, None, 'obj', 'tile'), may hold values from 0.19921875 to 2
- courant: float32 [2, 48, 8, 128], P(None, None, 'tile'), may hold values from -0.6 to 0.6
- insolation: float32 [8, 128], P('tile'), may hold values from 0.3 to 3
- region_mask: int32 [4, 8, 128], P('obj', 'tile'), may hold values 0 or 1
- measure_step: int32 [4], P('obj'), may hold values from 1 to 6
- snr_weight: float32 [12, 48], replicated, may hold values from 0.3 to 3
- diffusion_number: float32 [12, 47], replicated, may hold values from 0.1 to 2
- coupling: float32 [12, 12], replicated, may hold values from -1.75 to 1.75
- recombination: float32 [12], replicated, may hold values from 0.05 to 0.25
Outputs:
- state_adjoint: float32 [4, 12, 48, 8, 128], P('obj', None, None, 'tile')
- driver_grad: float32 [4, 6, 12, 48], P('obj')
The draws below stay inside these ranges and needn't reach their ends.
All inputs are finite; a program needn't handle non-finite values. No bound on the sum of `region_mask` on one device may be relied on, other than what follows from the above.
Results may differ from the reference program's by a relative error of at most 0.0003.
Values may be sent and summed in bfloat16 or wider, within the bound.
No kernel may reach another device: no remote copies, remote signals or barrier semaphores. Data moves between devices by JAX's collectives and lax.ppermute only.
A program may use at most 64 MiB of HBM per device.

```python
import math
import jax
import jax.numpy as jnp
from jax import lax

F = 12
L = 48
NLAT = 128
STEPS = 6
NOBJ = 4
NLON = 8
NCELLS = 1024


def with_ends(array, own_key, least, top_value):
    extent = array.shape
    spot = [jax.random.randint(jax.random.fold_in(own_key, axis), (), 0, extent[axis]) for axis in range(len(extent))]
    array = array.at[tuple(spot)].set(least)
    longest = extent.index(max(extent))
    spot[longest] = (spot[longest] + 1) % extent[longest]
    return array.at[tuple(spot)].set(top_value)


def block_scale(rng, shape, split, least, high):
    gain = 1.0
    for axis_at, blocks in split:
        heights = jax.random.uniform(jax.random.fold_in(jax.random.fold_in(rng, 6), axis_at), (blocks,), jnp.float32, least / len(split), high / len(split))
        gain = gain * jnp.repeat(jnp.exp(heights), shape[axis_at] // blocks).reshape((-1,) + (1,) * (len(shape) - 1 - axis_at))
    return gain


def centred(stream_key, dims, deviation, most, kind=jnp.bfloat16):
    result = jax.random.normal(stream_key, dims, jnp.float32) * deviation
    return jnp.minimum(jnp.maximum(result, -most), most).astype(kind)


def setup_inputs(seed: int = 0) -> dict:
    arg_keys = jax.random.split(jax.random.key(seed), 10)
    return {
        "checkpoints": jnp.clip(0.19921875 + 1.8007812 * jax.random.uniform(arg_keys[0], (STEPS, F, L, NLON, NLAT), jnp.float32) ** block_scale(arg_keys[0], (STEPS, F, L, NLON, NLAT), ((2, 4), (3, 8)), -0.2, 0.2), 0.19921875, 2.0).astype(jnp.bfloat16),
        "courant": jnp.clip(jax.random.uniform(arg_keys[1], (2, L, NLON, NLAT), jnp.float32, -0.6, 0.6) * block_scale(arg_keys[1], (2, L, NLON, NLAT), ((2, 8),), -0.4, 0.0), -0.6, 0.6),
        "insolation": jnp.clip(jnp.exp(math.log(3.0) - 2.3025851 * jax.random.uniform(arg_keys[2], (NLON, NLAT), jnp.float32) ** block_scale(arg_keys[2], (NLON, NLAT), ((0, 8),), -0.2, 0.2)), 0.3, 3.0),
        "region_mask": with_ends((jax.random.randint(arg_keys[3], (NOBJ, NLON, NLAT), 0, 2) < 1).astype(jnp.int32), jax.random.fold_in(arg_keys[3], 1), 0, 1),
        "measure_step": with_ends(jax.random.randint(arg_keys[4], (NOBJ,), 1, STEPS + 1), jax.random.fold_in(arg_keys[4], 1), 1, STEPS).astype(jnp.int32),
        "snr_weight": jnp.clip(jnp.exp(jax.random.uniform(arg_keys[5], (F, L), jnp.float32, math.log(0.3), math.log(3.0))), 0.3, 3.0),
        "diffusion_number": jnp.clip(jnp.exp(jax.random.uniform(arg_keys[6], (F, L - 1), jnp.float32, math.log(0.1), math.log(2.0))), 0.1, 2.0),
        "coupling": centred(arg_keys[7], (F, F), F ** -0.5, 1.75, jnp.float32),
        "recombination": jnp.clip(jnp.exp(jax.random.uniform(arg_keys[8], (F,), jnp.float32, math.log(0.05), math.log(0.25))), 0.05, 0.25),
    }


smoothing = 0.2

def advect_back(adjoint, courant):
    eastward = courant[0][None]
    northward = courant[1][None]
    flux = eastward * adjoint
    beside_all = jnp.roll(adjoint, -1, 2) + jnp.roll(adjoint, 1, 2)
    carried = jnp.roll(flux, -1, 2) - jnp.roll(flux, 1, 2)
    lat_pad = jnp.pad(adjoint, ((0, 0), (0, 0), (0, 0), (1, 1)))
    north_flux = jnp.pad(northward * adjoint, ((0, 0), (0, 0), (0, 0), (1, 1)))
    beside_all = beside_all + lat_pad[..., 2:] + lat_pad[..., :-2]
    carried = carried + north_flux[..., 2:] - north_flux[..., :-2]
    return (1.0 - 4.0 * smoothing) * adjoint + smoothing * beside_all + 0.5 * carried

def reference(checkpoints, courant, insolation, region_mask, measure_step, snr_weight, diffusion_number, coupling, recombination):
    below = jnp.pad(diffusion_number, ((0, 0), (1, 0)))
    above = jnp.pad(diffusion_number, ((0, 0), (0, 1)))
    middle = 1.0 + below + above

    def one_objective(index):
        impulse = region_mask[index].astype(jnp.float32)[None, None] * snr_weight[:, :, None, None]
        adjoint = jnp.zeros((F, L, NLON, NLAT), jnp.float32)
        grads = [None] * STEPS
        for back in range(STEPS):
            moment = STEPS - 1 - back
            arrive = (measure_step[index] == moment + 1).astype(jnp.float32)
            adjoint = adjoint + arrive * impulse
            advected = advect_back(adjoint, courant)
            solved = lax.linalg.tridiagonal_solve(-below, middle, -above, advected.reshape(F, L, NLON * NLAT)).reshape(F, L, NLON, NLAT)
            grads[moment] = jnp.einsum('flxy,xy->fl', solved, insolation, precision=lax.Precision.HIGHEST) / NCELLS
            state = checkpoints[moment].astype(jnp.float32)
            mixing = jnp.einsum('fg,flxy->glxy', coupling, solved, precision=lax.Precision.HIGHEST)
            adjoint = solved + mixing - 2.0 * recombination[:, None, None, None] * state * solved
        return (adjoint, jnp.stack(grads))
    adjoints, gradients = lax.map(one_objective, jnp.arange(NOBJ, dtype=jnp.int32))
    return (adjoints, gradients)
```

```python
import functools

import jax
import jax.numpy as jnp
from jax import lax
from jax.experimental import pallas as pl
from jax.experimental.pallas import tpu as pltpu
from jax.sharding import PartitionSpec as P

smoothing = 0.2
lanes = 128
quads = 4
window = lanes // quads
exact = lax.Precision.HIGHEST


def up(value, unit):
    return -(-value // unit) * unit


def lane_iota(shape):
    return lax.broadcasted_iota(jnp.int32, shape, len(shape) - 1)


def pack_kernel(dims, checkpoints, courant, insolation, region_mask, out, staged):
    steps, groups, part, tiles, own, halo, rows = dims
    ours = lax.axis_index("obj") * part
    total = rows["all"]
    for quad in range(quads):
        for moment in range(steps):
            for group in range(groups):
                at = (moment * groups + group) * part
                staged[quad, at : at + part, :] = checkpoints[moment, group * quads + quad].astype(jnp.float32)
    for way in range(2):
        wind = courant[way, pl.ds(ours, part), :]
        coarse = wind.astype(jnp.bfloat16).astype(jnp.float32)
        staged[2 * way, rows["wind"] : rows["wind"] + part, :] = coarse
        staged[2 * way + 1, rows["wind"] : rows["wind"] + part, :] = wind - coarse
    light = insolation[...]
    coarse = light.astype(jnp.bfloat16).astype(jnp.float32)
    middle = (light - coarse).astype(jnp.bfloat16).astype(jnp.float32)
    cells = [region_mask[...].astype(jnp.float32), coarse, middle, light - coarse - middle]
    for quad in range(quads):
        staged[quad, rows["cells"] : rows["cells"] + 1, :] = cells[quad]
        staged[quad, rows["cells"] + 1 : total, :] = jnp.zeros((total - rows["cells"] - 1, lanes), jnp.float32)
    source = jnp.concatenate([staged[quad].astype(jnp.bfloat16) for quad in range(quads)], axis=1)
    for tile in range(tiles):
        shape = (quads * lanes, lanes)
        row = lax.broadcasted_iota(jnp.int32, shape, 0)
        lane = lane_iota(shape)
        wanted = (lane // window) * lanes + own * tile - halo + lane % window
        inside = own * tile - halo + lane % window
        pick = (row == wanted) & (inside >= 0) & (inside < lanes)
        pick = jnp.where(pick, 1.0, 0.0).astype(jnp.bfloat16)
        out[tile] = jnp.dot(source, pick, preferred_element_type=jnp.float32).astype(jnp.bfloat16)


def spread(values, group):
    fields = values.shape[0]
    shape = (fields, lanes)
    field = lax.broadcasted_iota(jnp.int32, shape, 0)
    chosen = jnp.where(field == group * quads + lane_iota(shape) // window, 1.0, 0.0)
    return lax.dot_general(
        values, chosen, (((0,), (0,)), ((), ())), precision=exact, preferred_element_type=jnp.float32
    )


def everywhere(quarter):
    quarter = jnp.where(lane_iota(quarter.shape) < window, quarter, 0.0)
    axis = len(quarter.shape) - 1
    quarter = quarter + pltpu.roll(quarter, window, axis)
    return quarter + pltpu.roll(quarter, 2 * window, axis)


def main_kernel(
    dims,
    measure_step,
    arrived,
    snr_weight,
    diffusion,
    coupling,
    recombination,
    out,
    wide,
    adjoint,
    solving,
    coefs,
    snr,
    multiplier,
    inverse,
    mixing,
    loss,
    sums,
):
    steps, groups, part, tiles, own, halo, rows, out_rows = dims
    total = rows["all"]
    fields, levels = snr_weight.shape
    parts = levels // part
    tile = lax.axis_index("tile")
    cell = (tiles, lanes)
    lane = lane_iota(cell)
    spot = lane % window
    latitude = own * tile - halo + spot
    inside = jnp.where((latitude >= 0) & (latitude < lanes), 1.0, 0.0)

    for piece in range(parts):
        for longitude in range(tiles):
            at = (piece * tiles + longitude) * total
            wide[at : at + total, :] = arrived[piece, longitude].astype(jnp.float32)

    def stored(piece, row):
        return wide[pl.ds(piece * (tiles * total) + row, tiles, stride=total), :]

    me = lax.axis_index("obj")
    misc = stored(me, rows["cells"])
    mask = everywhere(misc)
    light = misc + pltpu.roll(misc, lanes - window, 1) + pltpu.roll(misc, lanes - 2 * window, 1)
    light = everywhere(pltpu.roll(light, lanes - window, 1))
    light = jnp.where((spot >= halo) & (spot < halo + own), light, 0.0)

    for level in range(levels):
        both = stored(level // part, rows["wind"] + level % part)
        both = both + pltpu.roll(both, lanes - window, 1)
        east = everywhere(both)
        north = everywhere(pltpu.roll(both, lanes - 2 * window, 1))
        coefs[level, 0] = pltpu.roll(smoothing + 0.5 * east, tiles - 1, 0) * inside
        coefs[level, 1] = pltpu.roll(smoothing - 0.5 * east, 1, 0) * inside
        coefs[level, 2] = pltpu.roll(smoothing + 0.5 * north, lanes - 1, 1) * inside
        coefs[level, 3] = pltpu.roll(smoothing - 0.5 * north, 1, 1) * inside
    centre = (1.0 - 4.0 * smoothing) * inside

    for group in range(groups):
        snr[group] = spread(snr_weight[...], group)
        number = spread(diffusion[...], group)
        below = jnp.zeros((1, lanes), jnp.float32)
        last = jnp.ones((1, lanes), jnp.float32)
        earlier = jnp.zeros((1, lanes), jnp.float32)
        for level in range(levels):
            above = number[level : level + 1] if level < levels - 1 else jnp.zeros((1, lanes), jnp.float32)
            now = (1.0 + below + above) * last - below * below * earlier
            part_inverse = last / now
            inverse[group, level : level + 1, :] = part_inverse
            multiplier[group, level + 1 : level + 2, :] = above * part_inverse
            earlier = last
            last = now
            below = above
        multiplier[group, 0:1, :] = jnp.zeros((1, lanes), jnp.float32)

    shape = (fields, fields)
    identity = jnp.where(lax.broadcasted_iota(jnp.int32, shape, 0) == lax.broadcasted_iota(jnp.int32, shape, 1), 1.0, 0.0)
    across = jnp.transpose(coupling[...] + identity)
    for group in range(groups):
        columns = spread(across, group)
        quarter = lane_iota((1, lanes)) // window
        for source in range(groups):
            for turn in range(quads):
                line = jnp.zeros((1, lanes), jnp.float32)
                for quad in range(quads):
                    field = source * quads + (quad - turn) % quads
                    line = jnp.where(quarter == quad, columns[field : field + 1], line)
                at = (group * groups + source) * quads + turn
                mixing[at] = jnp.broadcast_to(line, (8, lanes))
        loss[group] = jnp.broadcast_to(-2.0 * spread(recombination[...], group), (8, lanes))

    adjoint[...] = jnp.zeros_like(adjoint)
    block = 4 if levels % 4 == 0 else 1

    def step(back, carry):
        moment = steps - 1 - back
        scored = jnp.where(measure_step[0] == moment + 1, 1.0, 0.0) * mask

        def forward(at, before):
            before = list(before)
            for inner in range(block):
                level = at * block + inner
                for group in range(groups):
                    value = adjoint[level * groups + group] + scored * snr[group, pl.ds(level, 1), :]
                    moved = centre * value
                    moved = moved + coefs[level, 0] * pltpu.roll(value, tiles - 1, 0)
                    moved = moved + coefs[level, 1] * pltpu.roll(value, 1, 0)
                    moved = moved + coefs[level, 2] * pltpu.roll(value, lanes - 1, 1)
                    moved = moved + coefs[level, 3] * pltpu.roll(value, 1, 1)
                    moved = moved + multiplier[group, pl.ds(level, 1), :] * before[group]
                    before[group] = moved
                    solving[level * groups + group] = moved * inverse[group, pl.ds(level, 1), :]
            return tuple(before)

        nothing = tuple(jnp.zeros(cell, jnp.float32) for _ in range(groups))
        lax.fori_loop(0, levels // block, forward, nothing)

        def backward(at, after):
            after = list(after)
            for inner in range(block):
                level = levels - 1 - (at * block + inner)
                turned = []
                for group in range(groups):
                    value = solving[level * groups + group]
                    value = value + multiplier[group, pl.ds(level + 1, 1), :] * after[group]
                    after[group] = value
                    lit = jnp.sum(value * light, axis=0, keepdims=True)
                    sums[pl.ds((moment * groups + group) * levels + level, 1), :] = lit
                    turned.append([value] + [pltpu.roll(value, window * turn, 1) for turn in range(1, quads)])
                for group in range(groups):
                    state = stored(level // part, (moment * groups + group) * part + level % part)
                    result = loss[group, 0:1] * state * after[group]
                    for source in range(groups):
                        for turn in range(quads):
                            place = (group * groups + source) * quads + turn
                            result = result + mixing[place, 0:1] * turned[source][turn]
                    adjoint[level * groups + group] = result
            return tuple(after)

        lax.fori_loop(0, levels // block, backward, nothing)
        return carry

    lax.fori_loop(0, steps, step, 0)

    stack = tiles // quads
    short = levels // stack
    home = lane // own
    for group in range(groups):
        for level in range(short):
            whole = jnp.zeros(cell, jnp.float32)
            for high in range(stack):
                value = adjoint[(high * short + level) * groups + group]
                for quad in range(quads):
                    target = (high * quads + quad) * own
                    turned = pltpu.roll(value, (target - quad * window - halo) % lanes, 1)
                    whole = jnp.where(home == high * quads + quad, turned, whole)
            out[pl.ds(group * short + level, tiles, stride=out_rows), :] = whole
    shape = (8, lanes)
    chosen = jnp.where(lax.broadcasted_iota(jnp.int32, shape, 0) == lane_iota(shape) // window, 1.0, 0.0)
    base = groups * short
    half = steps // 2
    for moment in range(half):
        for group in range(groups):
            pair = []
            for at in (moment, moment + half):
                place = (at * groups + group) * levels
                pair.append(
                    lax.dot_general(
                        chosen,
                        sums[place : place + levels, :],
                        (((1,), (1,)), ((), ())),
                        precision=exact,
                        preferred_element_type=jnp.float32,
                    )[:quads]
                )
            gap = jnp.zeros((quads, lanes // 2 - levels), jnp.float32)
            line = jnp.concatenate([pair[0], gap, pair[1], gap], axis=1)
            for longitude in range(tiles):
                at = longitude * out_rows + base + moment * fields + group * quads
                out[at : at + quads, :] = line
    for longitude in range(tiles):
        at = longitude * out_rows + base + half * fields
        out[at : (longitude + 1) * out_rows, :] = jnp.zeros((out_rows - base - half * fields, lanes), jnp.float32)


def unpack_kernel(dims, arrived, state_adjoint, driver_grad):
    steps, groups, levels, fields, tiles, own, cells = dims
    stack = tiles // quads
    short = levels // stack
    base = groups * short
    half = steps // 2
    values = [arrived[tile, 0:base, :] for tile in range(tiles)]
    home = lane_iota((base, lanes)) // own
    apart = 1
    while apart < tiles:
        for low in range(tiles):
            if low & apart:
                continue
            first, second = values[low], values[low + apart]
            here = (home & apart) == 0
            values[low] = jnp.where(here, first, pltpu.roll(second, apart * own, 1))
            values[low + apart] = jnp.where(here, pltpu.roll(first, lanes - apart * own, 1), second)
        apart *= 2
    for high in range(stack):
        for quad in range(quads):
            for group in range(groups):
                at = (group * quads + quad) * levels + high * short
                state_adjoint[at : at + short, :] = values[high * quads + quad][group * short : (group + 1) * short]
    total = arrived[0, base : base + half * fields, :]
    for tile in range(1, tiles):
        total = total + arrived[tile, base : base + half * fields, :]
    total = total / cells
    late = pltpu.roll(total, lanes // 2, 1)
    for moment in range(half):
        driver_grad[moment] = total[moment * fields : (moment + 1) * fields, :levels]
        driver_grad[moment + half] = late[moment * fields : (moment + 1) * fields, :levels]


def per_device(
    checkpoints,
    courant,
    insolation,
    region_mask,
    measure_step,
    snr_weight,
    diffusion_number,
    coupling,
    recombination,
):
    steps, fields, part = checkpoints.shape[:3]
    levels = snr_weight.shape[1]
    tiles = lax.axis_size("tile")
    parts = levels // part
    groups = fields // quads
    own = lanes // tiles
    halo = (window - own) // 2
    rows = {"wind": steps * groups * part}
    rows["cells"] = rows["wind"] + part
    rows["all"] = up(rows["cells"] + 1, 16)
    total = rows["all"]
    short = levels // (tiles // quads)
    out_rows = up(groups * short + steps // 2 * fields, 8)
    limit = pltpu.CompilerParams(vmem_limit_bytes=48 * 2**20)
    in_vmem = pl.BlockSpec(memory_space=pltpu.VMEM)
    in_smem = pl.BlockSpec(memory_space=pltpu.SMEM)
    f32 = jnp.float32

    packed = pl.pallas_call(
        functools.partial(pack_kernel, (steps, groups, part, tiles, own, halo, rows)),
        out_shape=jax.ShapeDtypeStruct((tiles, total, lanes), jnp.bfloat16),
        in_specs=[in_vmem] * 4,
        out_specs=in_vmem,
        scratch_shapes=[pltpu.VMEM((quads, total, lanes), f32)],
        compiler_params=limit,
    )(
        checkpoints.reshape(steps, fields, part, lanes),
        courant.reshape(2, levels, lanes),
        insolation,
        region_mask.reshape(1, lanes),
    )
    strips = lax.all_to_all(packed, "tile", 0, 0, tiled=True)
    arrived = lax.all_gather(strips, "obj", axis=0, tiled=False)

    cell = (tiles, lanes)
    result = pl.pallas_call(
        functools.partial(main_kernel, (steps, groups, part, tiles, own, halo, rows, out_rows)),
        out_shape=jax.ShapeDtypeStruct((tiles * out_rows, lanes), f32),
        in_specs=[in_smem] + [in_vmem] * 5,
        out_specs=in_vmem,
        scratch_shapes=[
            pltpu.VMEM((parts * tiles * total, lanes), f32),
            pltpu.VMEM((levels * groups,) + cell, f32),
            pltpu.VMEM((levels * groups,) + cell, f32),
            pltpu.VMEM((levels, 4) + cell, f32),
            pltpu.VMEM((groups, levels, lanes), f32),
            pltpu.VMEM((groups, levels + 8, lanes), f32),
            pltpu.VMEM((groups, levels, lanes), f32),
            pltpu.VMEM((groups * groups * quads, 8, lanes), f32),
            pltpu.VMEM((groups, 8, lanes), f32),
            pltpu.VMEM((steps * groups * levels, lanes), f32),
        ],
        compiler_params=limit,
    )(
        measure_step,
        arrived,
        snr_weight,
        diffusion_number,
        coupling,
        recombination.reshape(fields, 1),
    )
    home = lax.all_to_all(result.reshape(tiles, out_rows, lanes), "tile", 0, 0, tiled=True)

    state_adjoint, driver_grad = pl.pallas_call(
        functools.partial(unpack_kernel, (steps, groups, levels, fields, tiles, own, tiles * lanes)),
        out_shape=(
            jax.ShapeDtypeStruct((fields * levels, lanes), f32),
            jax.ShapeDtypeStruct((steps, fields, levels), f32),
        ),
        in_specs=[in_vmem],
        out_specs=(in_vmem, in_vmem),
        compiler_params=limit,
    )(home)
    return (state_adjoint.reshape(1, fields, levels, 1, lanes), driver_grad[None])


def solution(mesh):
    return jax.shard_map(
        per_device,
        mesh=mesh,
        in_specs=(
            P(None, None, "obj", "tile", None),
            P(None, None, "tile", None),
            P("tile", None),
            P("obj", "tile", None),
            P("obj"),
            P(),
            P(),
            P(),
            P(),
        ),
        out_specs=(P("obj", None, None, "tile", None), P("obj", None, None, None)),
        check_vma=False,
    )
```

```python
import functools

import jax
import jax.numpy as jnp
from jax import lax
from jax.experimental import pallas as pl
from jax.experimental.pallas import tpu as pltpu
from jax.sharding import PartitionSpec as P

smoothing = 0.2
lanes = 128
quads = 4
window = lanes // quads
exact = lax.Precision.HIGHEST


def up(value, unit):
    return -(-value // unit) * unit


def lane_iota(shape):
    return lax.broadcasted_iota(jnp.int32, shape, len(shape) - 1)


def pack_kernel(dims, rows, spots, checkpoints, courant, insolation, region_mask, out, staged):
    steps, groups, part, tiles, own, halo = dims
    count = steps // 2
    ours = lax.axis_index("obj") * part
    total = sum(rows)
    for quad in range(quads):
        for back in range(steps):
            base = back * groups * part if back < count else rows[0] + (back - count) * groups * part
            for group in range(groups):
                at = base + group * part
                state = checkpoints[steps - 1 - back, group * quads + quad]
                staged[quad, at : at + part, :] = state.astype(jnp.float32)
    for way in range(2):
        wind = courant[way, pl.ds(ours, part), :]
        coarse = wind.astype(jnp.bfloat16).astype(jnp.float32)
        staged[2 * way, spots["wind"] : spots["wind"] + part, :] = coarse
        staged[2 * way + 1, spots["wind"] : spots["wind"] + part, :] = wind - coarse
    light = insolation[...]
    coarse = light.astype(jnp.bfloat16).astype(jnp.float32)
    middle = (light - coarse).astype(jnp.bfloat16).astype(jnp.float32)
    cells = [region_mask[...].astype(jnp.float32), coarse, middle, light - coarse - middle]
    ends = rows[0] + (steps - count) * groups * part
    for quad in range(quads):
        staged[quad, spots["cells"] : spots["cells"] + 1, :] = cells[quad]
        if spots["cells"] + 1 < rows[0]:
            rest = rows[0] - spots["cells"] - 1
            staged[quad, spots["cells"] + 1 : rows[0], :] = jnp.zeros((rest, lanes), jnp.float32)
        if ends < total:
            staged[quad, ends:total, :] = jnp.zeros((total - ends, lanes), jnp.float32)
    source = jnp.concatenate([staged[quad].astype(jnp.bfloat16) for quad in range(quads)], axis=1)
    for tile in range(tiles):
        shape = (quads * lanes, lanes)
        row = lax.broadcasted_iota(jnp.int32, shape, 0)
        lane = lane_iota(shape)
        wanted = (lane // window) * lanes + own * tile - halo + lane % window
        inside = own * tile - halo + lane % window
        pick = (row == wanted) & (inside >= 0) & (inside < lanes)
        pick = jnp.where(pick, 1.0, 0.0).astype(jnp.bfloat16)
        out[tile] = jnp.dot(source, pick, preferred_element_type=jnp.float32).astype(jnp.bfloat16)


def spread(values, group):
    fields = values.shape[0]
    shape = (fields, lanes)
    field = lax.broadcasted_iota(jnp.int32, shape, 0)
    chosen = jnp.where(field == group * quads + lane_iota(shape) // window, 1.0, 0.0)
    return lax.dot_general(
        values, chosen, (((0,), (0,)), ((), ())), precision=exact, preferred_element_type=jnp.float32
    )


def everywhere(quarter):
    quarter = jnp.where(lane_iota(quarter.shape) < window, quarter, 0.0)
    axis = len(quarter.shape) - 1
    quarter = quarter + pltpu.roll(quarter, window, axis)
    return quarter + pltpu.roll(quarter, 2 * window, axis)


def prepare_kernel(
    tiles, snr_weight, diffusion, coupling, recombination, snr, multiplier, inverse, mixing, loss, number, ratio
):
    fields, levels = snr_weight.shape
    groups = fields // quads
    cell = (tiles, lanes)
    for group in range(groups):
        spreaded = spread(snr_weight[...], group)
        for level in range(levels):
            snr[level * groups + group] = jnp.broadcast_to(spreaded[level : level + 1], cell)
        above = spread(diffusion[...], group)
        number[pl.ds(group, levels - 1, stride=8), :] = above
        number[pl.ds((levels - 1) * 8 + group, 1), :] = jnp.zeros((1, lanes), jnp.float32)

    valid = lax.broadcasted_iota(jnp.int32, (8, lanes), 0) < groups
    below = jnp.zeros((8, lanes), jnp.float32)
    last = jnp.ones((8, lanes), jnp.float32)
    earlier = jnp.zeros((8, lanes), jnp.float32)
    for level in range(levels):
        above = jnp.where(valid, number[level * 8 : level * 8 + 8, :], 0.0)
        now = (1.0 + below + above) * last - (below * below) * earlier
        turned = last / now
        ratio[level * 8 : level * 8 + 8, :] = turned
        number[level * 8 : level * 8 + 8, :] = above * turned
        earlier = last
        last = now
        below = above
    for group in range(groups):
        multiplier[group] = jnp.zeros(cell, jnp.float32)
        for level in range(levels):
            inverse[level * groups + group] = jnp.broadcast_to(ratio[level * 8 + group : level * 8 + group + 1, :], cell)
            multiplier[(level + 1) * groups + group] = jnp.broadcast_to(
                number[level * 8 + group : level * 8 + group + 1, :], cell
            )

    shape = (fields, fields)
    identity = jnp.where(lax.broadcasted_iota(jnp.int32, shape, 0) == lax.broadcasted_iota(jnp.int32, shape, 1), 1.0, 0.0)
    across = jnp.transpose(coupling[...] + identity)
    quarter = lane_iota((1, lanes)) // window
    for group in range(groups):
        columns = spread(across, group)
        for source in range(groups):
            for turn in range(quads):
                line = jnp.zeros((1, lanes), jnp.float32)
                for quad in range(quads):
                    field = source * quads + (quad - turn) % quads
                    line = jnp.where(quarter == quad, columns[field : field + 1], line)
                at = (group * groups + source) * quads + turn
                mixing[at] = jnp.broadcast_to(line, cell)
        loss[group] = jnp.broadcast_to(-2.0 * spread(recombination[...], group), cell)


def widen(dims, rows, pieces, wide):
    tiles = dims[3]
    me = lax.axis_index("obj")
    for apart, piece in enumerate(pieces):
        start = (me ^ apart) * (tiles * rows)
        for longitude in range(tiles):
            at = pl.multiple_of(start + longitude * rows, 8)
            wide[pl.ds(at, rows), :] = piece[longitude].astype(jnp.float32)


def steps_back(dims, rows, measure_step, first, count, mask, light, tables, wide, adjoint, coefs, sums, solving, lit):
    steps, groups, part, tiles, own, halo = dims
    snr, multiplier, inverse, mixing, loss = tables
    levels = adjoint.shape[0] // groups
    cell = (tiles, lanes)
    latitude = own * lax.axis_index("tile") - halo + lane_iota(cell) % window
    inside = jnp.where((latitude >= 0) & (latitude < lanes), 1.0, 0.0)
    centre = (1.0 - 4.0 * smoothing) * inside
    block = 12 if levels % 12 == 0 else 2
    nothing = tuple(jnp.zeros(cell, jnp.float32) for _ in range(groups))

    def step(back, carry):
        moment = first - back
        upcoming = jnp.where((measure_step[0] == moment) & (moment > 0), 1.0, 0.0)
        scored = upcoming * mask

        def forward(at, before):
            before = list(before)
            for inner in range(block):
                level = at * block + inner
                for group in range(groups):
                    row = level * groups + group
                    value = adjoint[row, 0:tiles]
                    moved = centre * value
                    moved = moved + coefs[level, 0] * adjoint[row, 1 : tiles + 1]
                    moved = moved + coefs[level, 1] * adjoint[row, tiles - 1 : 2 * tiles - 1]
                    moved = moved + coefs[level, 2] * pltpu.roll(value, lanes - 1, 1)
                    moved = moved + coefs[level, 3] * pltpu.roll(value, 1, 1)
                    moved = moved + multiplier[row] * before[group]
                    before[group] = moved
                    solving[row] = moved * inverse[row]
            return tuple(before)

        lax.fori_loop(0, levels // block, forward, nothing)

        def backward(at, after):
            after = list(after)
            for inner in range(0, block, 2):
                pair = [levels - 1 - (at * block + inner), levels - 2 - (at * block + inner)]
                turned = []
                states = []
                for level in pair:
                    shifted = []
                    state = []
                    for group in range(groups):
                        row = level * groups + group
                        value = solving[row] + multiplier[row + groups] * after[group]
                        after[group] = value
                        lit[pl.ds(pl.multiple_of(row * tiles, 8), tiles), :] = value * light
                        shifted.append([value] + [pltpu.roll(value, window * turn, 1) for turn in range(1, quads)])
                        start = (level // part) * (tiles * rows) + (back * groups + group) * part + level % part
                        state.append(wide[pl.ds(start, tiles, stride=rows), :])
                    turned.append(shifted)
                    states.append(state)
                for group in range(groups):
                    result = [
                        loss[group] * states[at_pair][group] * turned[at_pair][group][0]
                        + scored * snr[pair[at_pair] * groups + group]
                        for at_pair in range(2)
                    ]
                    for source in range(groups):
                        for turn in range(quads):
                            factor = mixing[(group * groups + source) * quads + turn]
                            for at_pair in range(2):
                                result[at_pair] = result[at_pair] + factor * turned[at_pair][source][turn]
                    for at_pair in range(2):
                        row = pair[at_pair] * groups + group
                        adjoint[row, 0:tiles] = result[at_pair]
                        adjoint[row, tiles : 2 * tiles] = result[at_pair]
            return tuple(after)

        lax.fori_loop(0, levels // block, backward, nothing)
        for eight in range(levels * groups // 8):
            total = lit[pl.ds(eight * 8 * tiles, 8, stride=tiles), :]
            for longitude in range(1, tiles):
                total = total + lit[pl.ds(eight * 8 * tiles + longitude, 8, stride=tiles), :]
            sums[pl.ds(pl.multiple_of(back * (levels * groups) + eight * 8, 8), 8), :] = total
        return carry

    lax.fori_loop(0, count, step, 0)


def early_kernel(dims, rows, spots, count, parts, measure_step, *refs):
    pieces, refs = refs[:parts], refs[parts:]
    tables, refs = refs[:5], refs[5:]
    adjoint, coefs, sums, cells, wide, solving, lit = refs
    steps, groups, part, tiles, own, halo = dims
    levels = adjoint.shape[0] // groups
    widen(dims, rows, pieces, wide)
    cell = (tiles, lanes)
    spot = lane_iota(cell) % window
    latitude = own * lax.axis_index("tile") - halo + spot
    inside = jnp.where((latitude >= 0) & (latitude < lanes), 1.0, 0.0)

    def stored(piece, row):
        return wide[pl.ds(piece * (tiles * rows) + row, tiles, stride=rows), :]

    misc = stored(lax.axis_index("obj"), spots["cells"])
    mask = everywhere(misc)
    light = misc + pltpu.roll(misc, lanes - window, 1) + pltpu.roll(misc, lanes - 2 * window, 1)
    light = everywhere(pltpu.roll(light, lanes - window, 1))
    light = jnp.where((spot >= halo) & (spot < halo + own), light, 0.0)
    cells[0] = mask
    cells[1] = light

    for level in range(levels):
        both = stored(level // part, spots["wind"] + level % part)
        both = both + pltpu.roll(both, lanes - window, 1)
        east = everywhere(both)
        north = everywhere(pltpu.roll(both, lanes - 2 * window, 1))
        coefs[level, 0] = pltpu.roll(smoothing + 0.5 * east, tiles - 1, 0) * inside
        coefs[level, 1] = pltpu.roll(smoothing - 0.5 * east, 1, 0) * inside
        coefs[level, 2] = pltpu.roll(smoothing + 0.5 * north, lanes - 1, 1) * inside
        coefs[level, 3] = pltpu.roll(smoothing - 0.5 * north, 1, 1) * inside

    scored = jnp.where(measure_step[0] == steps, 1.0, 0.0) * mask
    for row in range(levels * groups):
        begin = scored * tables[0][row]
        adjoint[row, 0:tiles] = begin
        adjoint[row, tiles : 2 * tiles] = begin
    steps_back(
        dims, rows, measure_step, steps - 1, count, mask, light, tables, wide, adjoint, coefs, sums, solving, lit
    )


def late_kernel(dims, rows, count, parts, out_rows, measure_step, *refs):
    pieces, refs = refs[:parts], refs[parts:]
    tables, refs = refs[:5], refs[5:]
    given, coefs, early_sums, cells, out, wide, adjoint, sums, solving, lit = refs
    steps, groups, part, tiles, own, halo = dims
    levels = adjoint.shape[0] // groups
    fields = groups * quads
    cell = (tiles, lanes)
    widen(dims, rows, pieces, wide)
    adjoint[...] = given[...]
    steps_back(
        dims,
        rows,
        measure_step,
        count - 1,
        count,
        cells[0],
        cells[1],
        tables,
        wide,
        adjoint,
        coefs,
        sums,
        solving,
        lit,
    )

    stack = tiles // quads
    short = levels // stack
    home = (lane_iota(cell) % window) // own
    for group in range(groups):
        for level in range(short):
            whole = jnp.zeros(cell, jnp.float32)
            for high in range(stack):
                value = adjoint[(high * short + level) * groups + group, 0:tiles]
                turned = pltpu.roll(value, (high * own - halo) % lanes, 1)
                whole = jnp.where(home == high, turned, whole)
            out[pl.ds(group * short + level, tiles, stride=out_rows), :] = whole
    shape = (8, lanes)
    chosen = jnp.where(lax.broadcasted_iota(jnp.int32, shape, 0) == lane_iota(shape) // window, 1.0, 0.0)
    base = groups * short
    gap = jnp.zeros((quads, lanes // 2 - levels), jnp.float32)
    for back in range(count):
        for group in range(groups):
            pair = []
            for table in (early_sums, sums):
                pair.append(
                    lax.dot_general(
                        chosen,
                        table[pl.ds(back * levels * groups + group, levels, stride=groups), :],
                        (((1,), (1,)), ((), ())),
                        precision=exact,
                        preferred_element_type=jnp.float32,
                    )[:quads]
                )
            line = jnp.concatenate([pair[0], gap, pair[1], gap], axis=1)
            for longitude in range(tiles):
                at = longitude * out_rows + base + back * fields + group * quads
                out[at : at + quads, :] = line
    for longitude in range(tiles):
        at = longitude * out_rows + base + count * fields
        if at < (longitude + 1) * out_rows:
            rest = (longitude + 1) * out_rows - at
            out[at : at + rest, :] = jnp.zeros((rest, lanes), jnp.float32)


def unpack_kernel(dims, arrived, state_adjoint, driver_grad):
    steps, groups, levels, fields, tiles, own, cells = dims
    stack = tiles // quads
    short = levels // stack
    base = groups * short
    half = steps // 2
    values = [arrived[tile, 0:base, :] for tile in range(tiles)]
    home = lane_iota((base, lanes)) // own
    apart = 1
    while apart < tiles:
        for low in range(tiles):
            if low & apart:
                continue
            first, second = values[low], values[low + apart]
            here = (home & apart) == 0
            values[low] = jnp.where(here, first, pltpu.roll(second, apart * own, 1))
            values[low + apart] = jnp.where(here, pltpu.roll(first, lanes - apart * own, 1), second)
        apart *= 2
    for high in range(stack):
        for quad in range(quads):
            for group in range(groups):
                at = (group * quads + quad) * levels + high * short
                state_adjoint[at : at + short, :] = values[quad * stack + high][group * short : (group + 1) * short]
    total = arrived[0, base : base + half * fields, :]
    for tile in range(1, tiles):
        total = total + arrived[tile, base : base + half * fields, :]
    total = total / cells
    late = pltpu.roll(total, lanes // 2, 1)
    for back in range(half):
        at = (steps - 1 - back) * fields
        driver_grad[at : at + fields, :] = total[back * fields : (back + 1) * fields, :levels]
        at = (half - 1 - back) * fields
        driver_grad[at : at + fields, :] = late[back * fields : (back + 1) * fields, :levels]


def across(value, bit):
    count = lax.axis_size("obj")
    return lax.ppermute(value, "obj", [(place, place ^ bit) for place in range(count)])


def gathered(mine):
    pieces = {0: mine}
    bits = []
    bit = 1
    while bit < lax.axis_size("obj"):
        bits.append(bit)
        bit *= 2
    for bit in bits[1:] + bits[:1]:
        for apart in sorted(pieces):
            pieces[apart ^ bit] = across(pieces[apart], bit)
    return [pieces[apart] for apart in range(len(pieces))]


def cost(micros):
    return pl.CostEstimate(flops=0, bytes_accessed=int(micros * 3_000_000), transcendentals=0)


def per_device(
    checkpoints,
    courant,
    insolation,
    region_mask,
    measure_step,
    snr_weight,
    diffusion_number,
    coupling,
    recombination,
):
    steps, fields, part = checkpoints.shape[:3]
    levels = snr_weight.shape[1]
    tiles = lax.axis_size("tile")
    parts = levels // part
    groups = fields // quads
    own = lanes // tiles
    halo = (window - own) // 2
    count = steps // 2
    dims = (steps, groups, part, tiles, own, halo)
    spots = {"wind": count * groups * part}
    spots["cells"] = spots["wind"] + part
    rows = (up(spots["cells"] + 1, 16), up((steps - count) * groups * part, 16))
    short = levels // (tiles // quads)
    out_rows = up(groups * short + count * fields, 8)
    limit = pltpu.CompilerParams(vmem_limit_bytes=48 * 2**20)
    in_vmem = pl.BlockSpec(memory_space=pltpu.VMEM)
    in_smem = pl.BlockSpec(memory_space=pltpu.SMEM)
    f32 = jnp.float32
    cell = (tiles, lanes)
    full = (levels * groups,) + cell

    packed = pl.pallas_call(
        functools.partial(pack_kernel, dims, rows, spots),
        out_shape=jax.ShapeDtypeStruct((tiles, sum(rows), lanes), jnp.bfloat16),
        in_specs=[in_vmem] * 4,
        out_specs=in_vmem,
        scratch_shapes=[pltpu.VMEM((quads, sum(rows), lanes), f32)],
        compiler_params=limit,
        cost_estimate=cost(1),
    )(
        checkpoints.reshape(steps, fields, part, lanes),
        courant.reshape(2, levels, lanes),
        insolation,
        region_mask.reshape(1, lanes),
    )
    strips = lax.all_to_all(packed, "tile", 0, 0, tiled=True)
    early = gathered(strips[:, : rows[0]])
    late = gathered(strips[:, rows[0] :])

    tables = pl.pallas_call(
        functools.partial(prepare_kernel, tiles),
        out_shape=(
            jax.ShapeDtypeStruct(full, f32),
            jax.ShapeDtypeStruct(((levels + 1) * groups,) + cell, f32),
            jax.ShapeDtypeStruct(full, f32),
            jax.ShapeDtypeStruct((groups * groups * quads,) + cell, f32),
            jax.ShapeDtypeStruct((groups,) + cell, f32),
        ),
        in_specs=[in_vmem] * 4,
        out_specs=(in_vmem,) * 5,
        scratch_shapes=[pltpu.VMEM((levels * 8, lanes), f32), pltpu.VMEM((levels * 8, lanes), f32)],
        compiler_params=limit,
        cost_estimate=cost(2),
    )(snr_weight, diffusion_number, coupling, recombination.reshape(fields, 1))

    work = [pltpu.VMEM(full, f32), pltpu.VMEM((levels * groups * tiles, lanes), f32)]
    known = pl.pallas_call(
        functools.partial(early_kernel, dims, rows[0], spots, count, parts),
        out_shape=(
            jax.ShapeDtypeStruct((levels * groups, 2 * tiles, lanes), f32),
            jax.ShapeDtypeStruct((levels, 4) + cell, f32),
            jax.ShapeDtypeStruct((count * groups * levels, lanes), f32),
            jax.ShapeDtypeStruct((2,) + cell, f32),
        ),
        in_specs=[in_smem] + [in_vmem] * (parts + 5),
        out_specs=(in_vmem,) * 4,
        scratch_shapes=[pltpu.VMEM((parts * tiles * rows[0], lanes), f32)] + work,
        compiler_params=limit,
        cost_estimate=cost(5),
    )(measure_step, *early, *tables)

    result = pl.pallas_call(
        functools.partial(late_kernel, dims, rows[1], steps - count, parts, out_rows),
        out_shape=jax.ShapeDtypeStruct((tiles * out_rows, lanes), f32),
        in_specs=[in_smem] + [in_vmem] * (parts + 9),
        out_specs=in_vmem,
        scratch_shapes=[
            pltpu.VMEM((parts * tiles * rows[1], lanes), f32),
            pltpu.VMEM((levels * groups, 2 * tiles, lanes), f32),
            pltpu.VMEM(((steps - count) * groups * levels, lanes), f32),
        ]
        + work,
        compiler_params=limit,
        cost_estimate=cost(5),
    )(measure_step, *late, *tables, *known)
    home = lax.all_to_all(result.reshape(tiles, out_rows, lanes), "tile", 0, 0, tiled=True)

    state_adjoint, driver_grad = pl.pallas_call(
        functools.partial(unpack_kernel, (steps, groups, levels, fields, tiles, own, tiles * lanes)),
        out_shape=(
            jax.ShapeDtypeStruct((fields * levels, lanes), f32),
            jax.ShapeDtypeStruct((steps * fields, levels), f32),
        ),
        in_specs=[in_vmem],
        out_specs=(in_vmem, in_vmem),
        compiler_params=limit,
    )(home)
    return (state_adjoint.reshape(1, fields, levels, 1, lanes), driver_grad.reshape(1, steps, fields, levels))


def solution(mesh):
    return jax.shard_map(
        per_device,
        mesh=mesh,
        in_specs=(
            P(None, None, "obj", "tile", None),
            P(None, None, "tile", None),
            P("tile", None),
            P("obj", "tile", None),
            P("obj"),
            P(),
            P(),
            P(),
            P(),
        ),
        out_specs=(P("obj", None, None, "tile", None), P("obj", None, None, None)),
        check_vma=False,
    )
```

```python
import functools

import jax
import jax.numpy as jnp
from jax import lax
from jax.experimental import pallas as pl
from jax.experimental.pallas import tpu as pltpu
from jax.sharding import PartitionSpec as P

smoothing = 0.2
lanes = 128
quads = 4
window = lanes // quads
exact = lax.Precision.HIGHEST
early_steps = 2


def up(value, unit):
    return -(-value // unit) * unit


def lane_iota(shape):
    return lax.broadcasted_iota(jnp.int32, shape, len(shape) - 1)


def pack_kernel(dims, rows, spots, *refs):
    outside, out, staged, inside, arrival = refs[:4], refs[4], refs[5], refs[6:10], refs[10]
    copies = [pltpu.make_async_copy(outside[i], inside[i], arrival.at[i]) for i in range(4)]
    for copy in copies:
        copy.start()
    for copy in copies:
        copy.wait()
    checkpoints, courant, insolation, region_mask = inside
    steps, groups, part, tiles, own, halo = dims
    count = early_steps
    ours = lax.axis_index("obj") * part
    total = sum(rows)
    for quad in range(quads):
        for back in range(steps):
            base = back * groups * part if back < count else rows[0] + (back - count) * groups * part
            for group in range(groups):
                at = base + group * part
                state = checkpoints[steps - 1 - back, group * quads + quad]
                staged[quad, at : at + part, :] = state.astype(jnp.float32)
    for way in range(2):
        wind = courant[way, pl.ds(ours, part), :]
        coarse = wind.astype(jnp.bfloat16).astype(jnp.float32)
        staged[2 * way, spots["wind"] : spots["wind"] + part, :] = coarse
        staged[2 * way + 1, spots["wind"] : spots["wind"] + part, :] = wind - coarse
    light = insolation[...]
    coarse = light.astype(jnp.bfloat16).astype(jnp.float32)
    middle = (light - coarse).astype(jnp.bfloat16).astype(jnp.float32)
    cells = [region_mask[...].astype(jnp.float32), coarse, middle, light - coarse - middle]
    ends = rows[0] + (steps - count) * groups * part
    for quad in range(quads):
        staged[quad, spots["cells"] : spots["cells"] + 1, :] = cells[quad]
        if spots["cells"] + 1 < rows[0]:
            rest = rows[0] - spots["cells"] - 1
            staged[quad, spots["cells"] + 1 : rows[0], :] = jnp.zeros((rest, lanes), jnp.float32)
        if ends < total:
            staged[quad, ends:total, :] = jnp.zeros((total - ends, lanes), jnp.float32)
    source = jnp.concatenate([staged[quad].astype(jnp.bfloat16) for quad in range(quads)], axis=1)
    for tile in range(tiles):
        shape = (quads * lanes, lanes)
        row = lax.broadcasted_iota(jnp.int32, shape, 0)
        lane = lane_iota(shape)
        wanted = (lane // window) * lanes + own * tile - halo + lane % window
        inside = own * tile - halo + lane % window
        pick = (row == wanted) & (inside >= 0) & (inside < lanes)
        pick = jnp.where(pick, 1.0, 0.0).astype(jnp.bfloat16)
        out[tile] = jnp.dot(source, pick, preferred_element_type=jnp.float32).astype(jnp.bfloat16)


def spread(values, group):
    fields = values.shape[0]
    shape = (fields, lanes)
    field = lax.broadcasted_iota(jnp.int32, shape, 0)
    chosen = jnp.where(field == group * quads + lane_iota(shape) // window, 1.0, 0.0)
    return lax.dot_general(
        values, chosen, (((0,), (0,)), ((), ())), precision=exact, preferred_element_type=jnp.float32
    )


def everywhere(quarter):
    quarter = jnp.where(lane_iota(quarter.shape) < window, quarter, 0.0)
    axis = len(quarter.shape) - 1
    quarter = quarter + pltpu.roll(quarter, window, axis)
    return quarter + pltpu.roll(quarter, 2 * window, axis)


def prepare_kernel(
    tiles, snr_weight, diffusion, coupling, recombination, snr, multiplier, inverse, mixing, loss, number, ratio
):
    fields, levels = snr_weight.shape
    groups = fields // quads
    cell = (tiles, lanes)
    for group in range(groups):
        spreaded = spread(snr_weight[...], group)
        for level in range(levels):
            snr[level * groups + group] = jnp.broadcast_to(spreaded[level : level + 1], cell)
        above = spread(diffusion[...], group)
        number[pl.ds(group, levels - 1, stride=8), :] = above
        number[pl.ds((levels - 1) * 8 + group, 1), :] = jnp.zeros((1, lanes), jnp.float32)

    valid = lax.broadcasted_iota(jnp.int32, (8, lanes), 0) < groups
    below = jnp.zeros((8, lanes), jnp.float32)
    last = jnp.ones((8, lanes), jnp.float32)
    earlier = jnp.zeros((8, lanes), jnp.float32)
    for level in range(levels):
        above = jnp.where(valid, number[level * 8 : level * 8 + 8, :], 0.0)
        now = (1.0 + below + above) * last - (below * below) * earlier
        turned = last / now
        ratio[level * 8 : level * 8 + 8, :] = turned
        number[level * 8 : level * 8 + 8, :] = above * turned
        earlier = last
        last = now
        below = above
    for group in range(groups):
        multiplier[group] = jnp.zeros(cell, jnp.float32)
        for level in range(levels):
            inverse[level * groups + group] = jnp.broadcast_to(ratio[level * 8 + group : level * 8 + group + 1, :], cell)
            multiplier[(level + 1) * groups + group] = jnp.broadcast_to(
                number[level * 8 + group : level * 8 + group + 1, :], cell
            )

    shape = (fields, fields)
    identity = jnp.where(lax.broadcasted_iota(jnp.int32, shape, 0) == lax.broadcasted_iota(jnp.int32, shape, 1), 1.0, 0.0)
    across = jnp.transpose(coupling[...] + identity)
    quarter = lane_iota((1, lanes)) // window
    for group in range(groups):
        columns = spread(across, group)
        for source in range(groups):
            for turn in range(quads):
                line = jnp.zeros((1, lanes), jnp.float32)
                for quad in range(quads):
                    field = source * quads + (quad - turn) % quads
                    line = jnp.where(quarter == quad, columns[field : field + 1], line)
                at = (group * groups + source) * quads + turn
                mixing[at] = jnp.broadcast_to(line, cell)
        loss[group] = jnp.broadcast_to(-2.0 * spread(recombination[...], group), cell)


def widen(dims, rows, pieces, wide):
    tiles = dims[3]
    me = lax.axis_index("obj")
    for apart, piece in enumerate(pieces):
        start = (me ^ apart) * (tiles * rows)
        for longitude in range(tiles):
            at = pl.multiple_of(start + longitude * rows, 8)
            wide[pl.ds(at, rows), :] = piece[longitude].astype(jnp.float32)


def steps_back(dims, rows, measure_step, first, count, mask, light, tables, wide, adjoint, coefs, sums, solving, lit):
    steps, groups, part, tiles, own, halo = dims
    snr, multiplier, inverse, mixing, loss = tables
    levels = adjoint.shape[0] // groups
    cell = (tiles, lanes)
    latitude = own * lax.axis_index("tile") - halo + lane_iota(cell) % window
    inside = jnp.where((latitude >= 0) & (latitude < lanes), 1.0, 0.0)
    centre = (1.0 - 4.0 * smoothing) * inside
    block = 12 if levels % 12 == 0 else levels
    together = 3 if block % 3 == 0 else 1
    nothing = tuple(jnp.zeros(cell, jnp.float32) for _ in range(groups))

    def step(back, carry):
        moment = first - back
        upcoming = jnp.where((measure_step[0] == moment) & (moment > 0), 1.0, 0.0)
        scored = upcoming * mask

        def forward(at, before):
            before = list(before)
            for inner in range(block):
                level = at * block + inner
                weight = [coefs[level, way] for way in range(4)]
                for group in range(groups):
                    row = level * groups + group
                    value = adjoint[row, 0:tiles]
                    moved = centre * value
                    moved = moved + weight[0] * adjoint[row, 1 : tiles + 1]
                    moved = moved + weight[1] * adjoint[row, tiles - 1 : 2 * tiles - 1]
                    moved = moved + weight[2] * pltpu.roll(value, lanes - 1, 1)
                    moved = moved + weight[3] * pltpu.roll(value, 1, 1)
                    moved = moved + multiplier[row] * before[group]
                    before[group] = moved
                    solving[row] = moved * inverse[row]
            return tuple(before)

        lax.fori_loop(0, levels // block, forward, nothing)

        def backward(at, after):
            after = list(after)
            for inner in range(0, block, together):
                pair = [levels - 1 - (at * block + inner + more) for more in range(together)]
                turned = []
                states = []
                for level in pair:
                    shifted = []
                    state = []
                    for group in range(groups):
                        row = level * groups + group
                        value = solving[row] + multiplier[row + groups] * after[group]
                        after[group] = value
                        lit[pl.ds(pl.multiple_of(row * tiles, 8), tiles), :] = value * light
                        shifted.append([value] + [pltpu.roll(value, window * turn, 1) for turn in range(1, quads)])
                        start = (level // part) * (tiles * rows) + (back * groups + group) * part + level % part
                        state.append(wide[pl.ds(start, tiles, stride=rows), :])
                    turned.append(shifted)
                    states.append(state)
                for group in range(groups):
                    result = [
                        loss[group] * states[at_pair][group] * turned[at_pair][group][0]
                        + scored * snr[pair[at_pair] * groups + group]
                        for at_pair in range(together)
                    ]
                    for source in range(groups):
                        for turn in range(quads):
                            factor = mixing[(group * groups + source) * quads + turn]
                            for at_pair in range(together):
                                result[at_pair] = result[at_pair] + factor * turned[at_pair][source][turn]
                    for at_pair in range(together):
                        row = pair[at_pair] * groups + group
                        adjoint[row, 0:tiles] = result[at_pair]
                        adjoint[row, tiles : 2 * tiles] = result[at_pair]
            return tuple(after)

        lax.fori_loop(0, levels // block, backward, nothing)
        for eight in range(levels * groups // 8):
            total = lit[pl.ds(eight * 8 * tiles, 8, stride=tiles), :]
            for longitude in range(1, tiles):
                total = total + lit[pl.ds(eight * 8 * tiles + longitude, 8, stride=tiles), :]
            sums[pl.ds(pl.multiple_of(back * (levels * groups) + eight * 8, 8), 8), :] = total
        return carry

    lax.fori_loop(0, count, step, 0)


def early_kernel(dims, rows, spots, count, parts, measure_step, *refs):
    pieces, refs = refs[:parts], refs[parts:]
    tables, refs = refs[:5], refs[5:]
    adjoint, coefs, sums, cells, wide, solving, lit = refs
    steps, groups, part, tiles, own, halo = dims
    levels = adjoint.shape[0] // groups
    widen(dims, rows, pieces, wide)
    cell = (tiles, lanes)
    spot = lane_iota(cell) % window
    latitude = own * lax.axis_index("tile") - halo + spot
    inside = jnp.where((latitude >= 0) & (latitude < lanes), 1.0, 0.0)

    def stored(piece, row):
        return wide[pl.ds(piece * (tiles * rows) + row, tiles, stride=rows), :]

    misc = stored(lax.axis_index("obj"), spots["cells"])
    mask = everywhere(misc)
    light = misc + pltpu.roll(misc, lanes - window, 1) + pltpu.roll(misc, lanes - 2 * window, 1)
    light = everywhere(pltpu.roll(light, lanes - window, 1))
    light = jnp.where((spot >= halo) & (spot < halo + own), light, 0.0)
    cells[0] = mask
    cells[1] = light

    for level in range(levels):
        both = stored(level // part, spots["wind"] + level % part)
        both = both + pltpu.roll(both, lanes - window, 1)
        east = everywhere(both)
        north = everywhere(pltpu.roll(both, lanes - 2 * window, 1))
        coefs[level, 0] = pltpu.roll(smoothing + 0.5 * east, tiles - 1, 0) * inside
        coefs[level, 1] = pltpu.roll(smoothing - 0.5 * east, 1, 0) * inside
        coefs[level, 2] = pltpu.roll(smoothing + 0.5 * north, lanes - 1, 1) * inside
        coefs[level, 3] = pltpu.roll(smoothing - 0.5 * north, 1, 1) * inside

    scored = jnp.where(measure_step[0] == steps, 1.0, 0.0) * mask
    for row in range(levels * groups):
        begin = scored * tables[0][row]
        adjoint[row, 0:tiles] = begin
        adjoint[row, tiles : 2 * tiles] = begin
    steps_back(
        dims, rows, measure_step, steps - 1, count, mask, light, tables, wide, adjoint, coefs, sums, solving, lit
    )


def late_kernel(dims, rows, count, parts, out_rows, measure_step, *refs):
    pieces, refs = refs[:parts], refs[parts:]
    tables, refs = refs[:5], refs[5:]
    given, coefs, early_sums, cells, out, wide, adjoint, sums, solving, lit = refs
    steps, groups, part, tiles, own, halo = dims
    levels = adjoint.shape[0] // groups
    fields = groups * quads
    cell = (tiles, lanes)
    widen(dims, rows, pieces, wide)
    adjoint[...] = given[...]
    steps_back(
        dims,
        rows,
        measure_step,
        count - 1,
        count,
        cells[0],
        cells[1],
        tables,
        wide,
        adjoint,
        coefs,
        sums,
        solving,
        lit,
    )

    stack = tiles // quads
    short = levels // stack
    home = (lane_iota(cell) % window) // own
    for group in range(groups):
        for level in range(short):
            whole = jnp.zeros(cell, jnp.float32)
            for high in range(stack):
                value = adjoint[(high * short + level) * groups + group, 0:tiles]
                turned = pltpu.roll(value, (high * own - halo) % lanes, 1)
                whole = jnp.where(home == high, turned, whole)
            out[pl.ds(group * short + level, tiles, stride=out_rows), :] = whole
    shape = (8, lanes)
    chosen = jnp.where(lax.broadcasted_iota(jnp.int32, shape, 0) == lane_iota(shape) // window, 1.0, 0.0)
    base = groups * short
    gap = jnp.zeros((quads, lanes // 2 - levels), jnp.float32)
    half = steps // 2

    def summed(back, group):
        early = steps - count
        table, place = (early_sums, back) if back < early else (sums, back - early)
        return lax.dot_general(
            chosen,
            table[pl.ds(place * levels * groups + group, levels, stride=groups), :],
            (((1,), (1,)), ((), ())),
            precision=exact,
            preferred_element_type=jnp.float32,
        )[:quads]

    for back in range(half):
        for group in range(groups):
            line = jnp.concatenate([summed(back, group), gap, summed(back + half, group), gap], axis=1)
            for longitude in range(tiles):
                at = longitude * out_rows + base + back * fields + group * quads
                out[at : at + quads, :] = line
    for longitude in range(tiles):
        at = longitude * out_rows + base + half * fields
        if at < (longitude + 1) * out_rows:
            rest = (longitude + 1) * out_rows - at
            out[at : at + rest, :] = jnp.zeros((rest, lanes), jnp.float32)


def unpack_kernel(dims, arrived, state_adjoint, driver_grad):
    steps, groups, levels, fields, tiles, own, cells = dims
    stack = tiles // quads
    short = levels // stack
    base = groups * short
    half = steps // 2
    values = [arrived[tile, 0:base, :] for tile in range(tiles)]
    home = lane_iota((base, lanes)) // own
    apart = 1
    while apart < tiles:
        for low in range(tiles):
            if low & apart:
                continue
            first, second = values[low], values[low + apart]
            here = (home & apart) == 0
            values[low] = jnp.where(here, first, pltpu.roll(second, apart * own, 1))
            values[low + apart] = jnp.where(here, pltpu.roll(first, lanes - apart * own, 1), second)
        apart *= 2
    for high in range(stack):
        for quad in range(quads):
            for group in range(groups):
                at = (group * quads + quad) * levels + high * short
                state_adjoint[at : at + short, :] = values[quad * stack + high][group * short : (group + 1) * short]
    total = arrived[0, base : base + half * fields, :]
    for tile in range(1, tiles):
        total = total + arrived[tile, base : base + half * fields, :]
    total = total / cells
    late = pltpu.roll(total, lanes // 2, 1)
    for back in range(half):
        at = (steps - 1 - back) * fields
        driver_grad[at : at + fields, :] = total[back * fields : (back + 1) * fields, :levels]
        at = (half - 1 - back) * fields
        driver_grad[at : at + fields, :] = late[back * fields : (back + 1) * fields, :levels]


def across(value, bit):
    count = lax.axis_size("obj")
    return lax.ppermute(value, "obj", [(place, place ^ bit) for place in range(count)])


def hold(value, *after):
    def nothing(*refs):
        pass

    anywhere = pl.BlockSpec(memory_space=pl.ANY)
    return pl.pallas_call(
        nothing,
        out_shape=jax.ShapeDtypeStruct(value.shape, value.dtype),
        in_specs=[anywhere] * (1 + len(after)),
        out_specs=anywhere,
        input_output_aliases={0: 0},
    )(value, *after)


def over_chips(mine):
    pieces = {0: mine}
    bit = 2
    while bit < lax.axis_size("obj"):
        for apart in sorted(pieces):
            pieces[apart ^ bit] = across(pieces[apart], bit)
        bit *= 2
    return pieces


def over_cores(pieces):
    if lax.axis_size("obj") > 1:
        for apart in sorted(pieces):
            pieces[apart ^ 1] = across(pieces[apart], 1)
    return [pieces[apart] for apart in range(len(pieces))]


def cost(micros):
    return pl.CostEstimate(flops=0, bytes_accessed=int(micros * 3_000_000), transcendentals=0)


def per_device(
    checkpoints,
    courant,
    insolation,
    region_mask,
    measure_step,
    snr_weight,
    diffusion_number,
    coupling,
    recombination,
):
    steps, fields, part = checkpoints.shape[:3]
    levels = snr_weight.shape[1]
    tiles = lax.axis_size("tile")
    parts = levels // part
    groups = fields // quads
    own = lanes // tiles
    halo = (window - own) // 2
    count = early_steps
    dims = (steps, groups, part, tiles, own, halo)
    spots = {"wind": count * groups * part}
    spots["cells"] = spots["wind"] + part
    rows = (up(spots["cells"] + 1, 8), up((steps - count) * groups * part, 8))
    short = levels // (tiles // quads)
    out_rows = up(groups * short + steps // 2 * fields, 8)
    limit = pltpu.CompilerParams(vmem_limit_bytes=48 * 2**20)
    in_vmem = pl.BlockSpec(memory_space=pltpu.VMEM)
    in_smem = pl.BlockSpec(memory_space=pltpu.SMEM)
    f32 = jnp.float32
    cell = (tiles, lanes)
    full = (levels * groups,) + cell

    packed = pl.pallas_call(
        functools.partial(pack_kernel, dims, rows, spots),
        out_shape=jax.ShapeDtypeStruct((tiles, sum(rows), lanes), jnp.bfloat16),
        in_specs=[pl.BlockSpec(memory_space=pltpu.HBM)] * 4,
        out_specs=in_vmem,
        scratch_shapes=[
            pltpu.VMEM((quads, sum(rows), lanes), f32),
            pltpu.VMEM((steps, fields, part, lanes), checkpoints.dtype),
            pltpu.VMEM((2, levels, lanes), f32),
            pltpu.VMEM((1, lanes), f32),
            pltpu.VMEM((1, lanes), jnp.int32),
            pltpu.SemaphoreType.DMA((4,)),
        ],
        compiler_params=pltpu.CompilerParams(vmem_limit_bytes=64 * 2**20),
        cost_estimate=cost(1),
    )(
        checkpoints.reshape(steps, fields, part, lanes),
        courant.reshape(2, levels, lanes),
        insolation,
        region_mask.reshape(1, lanes),
    )
    tables = pl.pallas_call(
        functools.partial(prepare_kernel, tiles),
        out_shape=(
            jax.ShapeDtypeStruct(full, f32),
            jax.ShapeDtypeStruct(((levels + 1) * groups,) + cell, f32),
            jax.ShapeDtypeStruct(full, f32),
            jax.ShapeDtypeStruct((groups * groups * quads,) + cell, f32),
            jax.ShapeDtypeStruct((groups,) + cell, f32),
        ),
        in_specs=[in_vmem] * 4,
        out_specs=(in_vmem,) * 5,
        scratch_shapes=[pltpu.VMEM((levels * 8, lanes), f32), pltpu.VMEM((levels * 8, lanes), f32)],
        compiler_params=limit,
        cost_estimate=cost(2),
    )(snr_weight, diffusion_number, coupling, recombination.reshape(fields, 1))

    strips = lax.all_to_all(packed, "tile", 0, 0, tiled=True)
    early = over_chips(strips[:, : rows[0]])
    late = over_chips(hold(strips[:, rows[0] :], *[early[apart] for apart in sorted(early)[1:]], tables[4]))
    early = over_cores(early)

    work = [pltpu.VMEM(full, f32), pltpu.VMEM((levels * groups * tiles, lanes), f32)]
    known = pl.pallas_call(
        functools.partial(early_kernel, dims, rows[0], spots, count, parts),
        out_shape=(
            jax.ShapeDtypeStruct((levels * groups, 2 * tiles, lanes), f32),
            jax.ShapeDtypeStruct((levels, 4) + cell, f32),
            jax.ShapeDtypeStruct((count * groups * levels, lanes), f32),
            jax.ShapeDtypeStruct((2,) + cell, f32),
        ),
        in_specs=[in_smem] + [in_vmem] * (parts + 5),
        out_specs=(in_vmem,) * 4,
        scratch_shapes=[pltpu.VMEM((parts * tiles * rows[0], lanes), f32)] + work,
        compiler_params=limit,
        cost_estimate=cost(5),
    )(measure_step, *early, *tables)

    late = over_cores({apart: hold(late[apart], known[3]) if apart else late[apart] for apart in late})
    result = pl.pallas_call(
        functools.partial(late_kernel, dims, rows[1], steps - count, parts, out_rows),
        out_shape=jax.ShapeDtypeStruct((tiles * out_rows, lanes), f32),
        in_specs=[in_smem] + [in_vmem] * (parts + 9),
        out_specs=in_vmem,
        scratch_shapes=[
            pltpu.VMEM((parts * tiles * rows[1], lanes), f32),
            pltpu.VMEM((levels * groups, 2 * tiles, lanes), f32),
            pltpu.VMEM(((steps - count) * groups * levels, lanes), f32),
        ]
        + work,
        compiler_params=limit,
        cost_estimate=cost(5),
    )(measure_step, *late, *tables, *known)
    home = lax.all_to_all(result.reshape(tiles, out_rows, lanes), "tile", 0, 0, tiled=True)

    state_adjoint, driver_grad = pl.pallas_call(
        functools.partial(unpack_kernel, (steps, groups, levels, fields, tiles, own, tiles * lanes)),
        out_shape=(
            jax.ShapeDtypeStruct((fields * levels, lanes), f32),
            jax.ShapeDtypeStruct((steps * fields, levels), f32),
        ),
        in_specs=[in_vmem],
        out_specs=(in_vmem, in_vmem),
        compiler_params=limit,
    )(home)
    return (state_adjoint.reshape(1, fields, levels, 1, lanes), driver_grad.reshape(1, steps, fields, levels))


def solution(mesh):
    return jax.shard_map(
        per_device,
        mesh=mesh,
        in_specs=(
            P(None, None, "obj", "tile", None),
            P(None, None, "tile", None),
            P("tile", None),
            P("obj", "tile", None),
            P("obj"),
            P(),
            P(),
            P(),
            P(),
        ),
        out_specs=(P("obj", None, None, "tile", None), P("obj", None, None, None)),
        check_vma=False,
    )
```

```python
import functools

import jax
import jax.numpy as jnp
from jax import lax
from jax.experimental import pallas as pl
from jax.experimental.pallas import tpu as pltpu
from jax.sharding import PartitionSpec as P

smoothing = 0.2
lanes = 128
quads = 4
window = lanes // quads
exact = lax.Precision.HIGHEST
early_steps = 2


def up(value, unit):
    return -(-value // unit) * unit


def lane_iota(shape):
    return lax.broadcasted_iota(jnp.int32, shape, len(shape) - 1)


def pack_kernel(dims, rows, spots, *refs):
    outside, out, staged, inside, arrival = refs[:4], refs[4], refs[5], refs[6:10], refs[10]
    copies = [pltpu.make_async_copy(outside[i], inside[i], arrival.at[i]) for i in range(4)]
    for copy in copies:
        copy.start()
    for copy in copies:
        copy.wait()
    checkpoints, courant, insolation, region_mask = inside
    steps, groups, part, tiles, own, halo = dims
    count = early_steps
    ours = lax.axis_index("obj") * part
    total = sum(rows)
    for quad in range(quads):
        for back in range(steps):
            base = back * groups * part if back < count else rows[0] + (back - count) * groups * part
            for group in range(groups):
                at = base + group * part
                state = checkpoints[steps - 1 - back, group * quads + quad]
                staged[quad, at : at + part, :] = state.astype(jnp.float32)
    for way in range(2):
        wind = courant[way, pl.ds(ours, part), :]
        coarse = wind.astype(jnp.bfloat16).astype(jnp.float32)
        staged[2 * way, spots["wind"] : spots["wind"] + part, :] = coarse
        staged[2 * way + 1, spots["wind"] : spots["wind"] + part, :] = wind - coarse
    light = insolation[...]
    coarse = light.astype(jnp.bfloat16).astype(jnp.float32)
    middle = (light - coarse).astype(jnp.bfloat16).astype(jnp.float32)
    cells = [region_mask[...].astype(jnp.float32), coarse, middle, light - coarse - middle]
    ends = rows[0] + (steps - count) * groups * part
    for quad in range(quads):
        staged[quad, spots["cells"] : spots["cells"] + 1, :] = cells[quad]
        if spots["cells"] + 1 < rows[0]:
            rest = rows[0] - spots["cells"] - 1
            staged[quad, spots["cells"] + 1 : rows[0], :] = jnp.zeros((rest, lanes), jnp.float32)
        if ends < total:
            staged[quad, ends:total, :] = jnp.zeros((total - ends, lanes), jnp.float32)
    source = jnp.concatenate([staged[quad].astype(jnp.bfloat16) for quad in range(quads)], axis=1)
    for tile in range(tiles):
        shape = (quads * lanes, lanes)
        row = lax.broadcasted_iota(jnp.int32, shape, 0)
        lane = lane_iota(shape)
        wanted = (lane // window) * lanes + own * tile - halo + lane % window
        inside = own * tile - halo + lane % window
        pick = (row == wanted) & (inside >= 0) & (inside < lanes)
        pick = jnp.where(pick, 1.0, 0.0).astype(jnp.bfloat16)
        out[tile] = jnp.dot(source, pick, preferred_element_type=jnp.float32).astype(jnp.bfloat16)


def spread(values, group):
    fields = values.shape[0]
    shape = (fields, lanes)
    field = lax.broadcasted_iota(jnp.int32, shape, 0)
    chosen = jnp.where(field == group * quads + lane_iota(shape) // window, 1.0, 0.0)
    return lax.dot_general(
        values, chosen, (((0,), (0,)), ((), ())), precision=exact, preferred_element_type=jnp.float32
    )


def everywhere(quarter):
    quarter = jnp.where(lane_iota(quarter.shape) < window, quarter, 0.0)
    axis = len(quarter.shape) - 1
    quarter = quarter + pltpu.roll(quarter, window, axis)
    return quarter + pltpu.roll(quarter, 2 * window, axis)


def prepare_kernel(
    tiles, snr_weight, diffusion, coupling, recombination, snr, multiplier, inverse, mixing, loss, number, ratio
):
    fields, levels = snr_weight.shape
    groups = fields // quads
    cell = (tiles, lanes)
    for group in range(groups):
        spreaded = spread(snr_weight[...], group)
        for level in range(levels):
            snr[level * groups + group] = jnp.broadcast_to(spreaded[level : level + 1], cell)
        above = spread(diffusion[...], group)
        number[pl.ds(group, levels - 1, stride=8), :] = above
        number[pl.ds((levels - 1) * 8 + group, 1), :] = jnp.zeros((1, lanes), jnp.float32)

    valid = lax.broadcasted_iota(jnp.int32, (8, lanes), 0) < groups
    below = jnp.zeros((8, lanes), jnp.float32)
    last = jnp.ones((8, lanes), jnp.float32)
    earlier = jnp.zeros((8, lanes), jnp.float32)
    for level in range(levels):
        above = jnp.where(valid, number[level * 8 : level * 8 + 8, :], 0.0)
        now = (1.0 + below + above) * last - (below * below) * earlier
        turned = last / now
        ratio[level * 8 : level * 8 + 8, :] = turned
        number[level * 8 : level * 8 + 8, :] = above * turned
        earlier = last
        last = now
        below = above
    for group in range(groups):
        multiplier[group] = jnp.zeros(cell, jnp.float32)
        for level in range(levels):
            inverse[level * groups + group] = jnp.broadcast_to(ratio[level * 8 + group : level * 8 + group + 1, :], cell)
            multiplier[(level + 1) * groups + group] = jnp.broadcast_to(
                number[level * 8 + group : level * 8 + group + 1, :], cell
            )

    shape = (fields, fields)
    identity = jnp.where(lax.broadcasted_iota(jnp.int32, shape, 0) == lax.broadcasted_iota(jnp.int32, shape, 1), 1.0, 0.0)
    across = jnp.transpose(coupling[...] + identity)
    quarter = lane_iota((1, lanes)) // window
    for group in range(groups):
        columns = spread(across, group)
        for source in range(groups):
            for turn in range(quads):
                line = jnp.zeros((1, lanes), jnp.float32)
                for quad in range(quads):
                    field = source * quads + (quad - turn) % quads
                    line = jnp.where(quarter == quad, columns[field : field + 1], line)
                at = (group * groups + source) * quads + turn
                mixing[at] = jnp.broadcast_to(line, cell)
        loss[group] = jnp.broadcast_to(-2.0 * spread(recombination[...], group), cell)


def widen(dims, rows, pieces, wide):
    tiles = dims[3]
    me = lax.axis_index("obj")
    for apart, piece in enumerate(pieces):
        start = (me ^ apart) * (tiles * rows)
        for longitude in range(tiles):
            at = pl.multiple_of(start + longitude * rows, 8)
            wide[pl.ds(at, rows), :] = piece[longitude].astype(jnp.float32)


def steps_back(dims, rows, measure_step, first, count, mask, light, tables, wide, adjoint, coefs, sums, solving, lit):
    steps, groups, part, tiles, own, halo = dims
    snr, multiplier, inverse, mixing, loss = tables
    levels = adjoint.shape[0] // groups
    cell = (tiles, lanes)
    latitude = own * lax.axis_index("tile") - halo + lane_iota(cell) % window
    inside = jnp.where((latitude >= 0) & (latitude < lanes), 1.0, 0.0)
    centre = (1.0 - 4.0 * smoothing) * inside
    block = 12 if levels % 12 == 0 else levels
    together = 3 if block % 3 == 0 else 1
    nothing = tuple(jnp.zeros(cell, jnp.float32) for _ in range(groups))

    def step(back, carry):
        moment = first - back
        upcoming = jnp.where((measure_step[0] == moment) & (moment > 0), 1.0, 0.0)
        scored = upcoming * mask

        def forward(at, before):
            before = list(before)
            for inner in range(block):
                level = at * block + inner
                weight = [coefs[level, way] for way in range(4)]
                for group in range(groups):
                    row = level * groups + group
                    value = adjoint[row, 0:tiles]
                    moved = centre * value
                    moved = moved + weight[0] * adjoint[row, 1 : tiles + 1]
                    moved = moved + weight[1] * adjoint[row, tiles - 1 : 2 * tiles - 1]
                    moved = moved + weight[2] * pltpu.roll(value, lanes - 1, 1)
                    moved = moved + weight[3] * pltpu.roll(value, 1, 1)
                    moved = moved + multiplier[row] * before[group]
                    before[group] = moved
                    solving[row] = moved * inverse[row]
            return tuple(before)

        lax.fori_loop(0, levels // block, forward, nothing)

        def backward(at, after):
            after = list(after)
            for inner in range(0, block, together):
                pair = [levels - 1 - (at * block + inner + more) for more in range(together)]
                turned = []
                states = []
                for level in pair:
                    shifted = []
                    state = []
                    for group in range(groups):
                        row = level * groups + group
                        value = solving[row] + multiplier[row + groups] * after[group]
                        after[group] = value
                        lit[pl.ds(pl.multiple_of(row * tiles, 8), tiles), :] = value * light
                        shifted.append([value] + [pltpu.roll(value, window * turn, 1) for turn in range(1, quads)])
                        start = (level // part) * (tiles * rows) + (back * groups + group) * part + level % part
                        state.append(wide[pl.ds(start, tiles, stride=rows), :])
                    turned.append(shifted)
                    states.append(state)
                for group in range(groups):
                    result = [
                        loss[group] * states[at_pair][group] * turned[at_pair][group][0]
                        + scored * snr[pair[at_pair] * groups + group]
                        for at_pair in range(together)
                    ]
                    for source in range(groups):
                        for turn in range(quads):
                            factor = mixing[(group * groups + source) * quads + turn]
                            for at_pair in range(together):
                                result[at_pair] = result[at_pair] + factor * turned[at_pair][source][turn]
                    for at_pair in range(together):
                        row = pair[at_pair] * groups + group
                        adjoint[row, 0:tiles] = result[at_pair]
                        adjoint[row, tiles : 2 * tiles] = result[at_pair]
            return tuple(after)

        lax.fori_loop(0, levels // block, backward, nothing)
        for eight in range(levels * groups // 8):
            total = lit[pl.ds(eight * 8 * tiles, 8, stride=tiles), :]
            for longitude in range(1, tiles):
                total = total + lit[pl.ds(eight * 8 * tiles + longitude, 8, stride=tiles), :]
            sums[pl.ds(pl.multiple_of(back * (levels * groups) + eight * 8, 8), 8), :] = total
        return carry

    lax.fori_loop(0, count, step, 0)


def early_kernel(dims, rows, spots, count, parts, measure_step, *refs):
    pieces, refs = refs[:parts], refs[parts:]
    tables, refs = refs[:5], refs[5:]
    adjoint, coefs, sums, cells, wide, solving, lit = refs
    steps, groups, part, tiles, own, halo = dims
    levels = adjoint.shape[0] // groups
    widen(dims, rows, pieces, wide)
    cell = (tiles, lanes)
    spot = lane_iota(cell) % window
    latitude = own * lax.axis_index("tile") - halo + spot
    inside = jnp.where((latitude >= 0) & (latitude < lanes), 1.0, 0.0)

    def stored(piece, row):
        return wide[pl.ds(piece * (tiles * rows) + row, tiles, stride=rows), :]

    misc = stored(lax.axis_index("obj"), spots["cells"])
    mask = everywhere(misc)
    light = misc + pltpu.roll(misc, lanes - window, 1) + pltpu.roll(misc, lanes - 2 * window, 1)
    light = everywhere(pltpu.roll(light, lanes - window, 1))
    light = jnp.where((spot >= halo) & (spot < halo + own), light, 0.0)
    cells[0] = mask
    cells[1] = light

    for level in range(levels):
        both = stored(level // part, spots["wind"] + level % part)
        both = both + pltpu.roll(both, lanes - window, 1)
        east = everywhere(both)
        north = everywhere(pltpu.roll(both, lanes - 2 * window, 1))
        coefs[level, 0] = pltpu.roll(smoothing + 0.5 * east, tiles - 1, 0) * inside
        coefs[level, 1] = pltpu.roll(smoothing - 0.5 * east, 1, 0) * inside
        coefs[level, 2] = pltpu.roll(smoothing + 0.5 * north, lanes - 1, 1) * inside
        coefs[level, 3] = pltpu.roll(smoothing - 0.5 * north, 1, 1) * inside

    scored = jnp.where(measure_step[0] == steps, 1.0, 0.0) * mask
    for row in range(levels * groups):
        begin = scored * tables[0][row]
        adjoint[row, 0:tiles] = begin
        adjoint[row, tiles : 2 * tiles] = begin
    steps_back(
        dims, rows, measure_step, steps - 1, count, mask, light, tables, wide, adjoint, coefs, sums, solving, lit
    )


def late_kernel(dims, rows, count, parts, out_rows, measure_step, *refs):
    pieces, refs = refs[:parts], refs[parts:]
    tables, refs = refs[:5], refs[5:]
    given, coefs, early_sums, cells, out, wide, adjoint, sums, solving, lit = refs
    steps, groups, part, tiles, own, halo = dims
    levels = adjoint.shape[0] // groups
    fields = groups * quads
    cell = (tiles, lanes)
    widen(dims, rows, pieces, wide)
    adjoint[...] = given[...]
    steps_back(
        dims,
        rows,
        measure_step,
        count - 1,
        count,
        cells[0],
        cells[1],
        tables,
        wide,
        adjoint,
        coefs,
        sums,
        solving,
        lit,
    )

    stack = tiles // quads
    short = levels // stack
    home = (lane_iota(cell) % window) // own
    for group in range(groups):
        for level in range(short):
            whole = jnp.zeros(cell, jnp.float32)
            for high in range(stack):
                value = adjoint[(high * short + level) * groups + group, 0:tiles]
                turned = pltpu.roll(value, (high * own - halo) % lanes, 1)
                whole = jnp.where(home == high, turned, whole)
            out[pl.ds(group * short + level, tiles, stride=out_rows), :] = whole
    shape = (8, lanes)
    chosen = jnp.where(lax.broadcasted_iota(jnp.int32, shape, 0) == lane_iota(shape) // window, 1.0, 0.0)
    base = groups * short
    gap = jnp.zeros((quads, lanes // 2 - levels), jnp.float32)
    half = steps // 2

    def summed(back, group):
        early = steps - count
        table, place = (early_sums, back) if back < early else (sums, back - early)
        return lax.dot_general(
            chosen,
            table[pl.ds(place * levels * groups + group, levels, stride=groups), :],
            (((1,), (1,)), ((), ())),
            precision=exact,
            preferred_element_type=jnp.float32,
        )[:quads]

    for back in range(half):
        for group in range(groups):
            line = jnp.concatenate([summed(back, group), gap, summed(back + half, group), gap], axis=1)
            for longitude in range(tiles):
                at = longitude * out_rows + base + back * fields + group * quads
                out[at : at + quads, :] = line
    for longitude in range(tiles):
        at = longitude * out_rows + base + half * fields
        if at < (longitude + 1) * out_rows:
            rest = (longitude + 1) * out_rows - at
            out[at : at + rest, :] = jnp.zeros((rest, lanes), jnp.float32)


def unpack_kernel(dims, arrived, state_adjoint, driver_grad):
    steps, groups, levels, fields, tiles, own, cells = dims
    stack = tiles // quads
    short = levels // stack
    base = groups * short
    half = steps // 2
    values = [arrived[tile, 0:base, :] for tile in range(tiles)]
    home = lane_iota((base, lanes)) // own
    apart = 1
    while apart < tiles:
        for low in range(tiles):
            if low & apart:
                continue
            first, second = values[low], values[low + apart]
            here = (home & apart) == 0
            values[low] = jnp.where(here, first, pltpu.roll(second, apart * own, 1))
            values[low + apart] = jnp.where(here, pltpu.roll(first, lanes - apart * own, 1), second)
        apart *= 2
    for high in range(stack):
        for quad in range(quads):
            for group in range(groups):
                at = (group * quads + quad) * levels + high * short
                state_adjoint[at : at + short, :] = values[quad * stack + high][group * short : (group + 1) * short]
    total = arrived[0, base : base + half * fields, :]
    for tile in range(1, tiles):
        total = total + arrived[tile, base : base + half * fields, :]
    total = total / cells
    late = pltpu.roll(total, lanes // 2, 1)
    for back in range(half):
        at = (steps - 1 - back) * fields
        driver_grad[at : at + fields, :] = total[back * fields : (back + 1) * fields, :levels]
        at = (half - 1 - back) * fields
        driver_grad[at : at + fields, :] = late[back * fields : (back + 1) * fields, :levels]


def across(value, bit):
    count = lax.axis_size("obj")
    return lax.ppermute(value, "obj", [(place, place ^ bit) for place in range(count)])


def hold(value, *after):
    def nothing(*refs):
        pass

    near = pl.BlockSpec(memory_space=pltpu.VMEM)
    return pl.pallas_call(
        nothing,
        out_shape=jax.ShapeDtypeStruct(value.shape, value.dtype),
        in_specs=[near] * (1 + len(after)),
        out_specs=near,
        input_output_aliases={0: 0},
        compiler_params=pltpu.CompilerParams(vmem_limit_bytes=2**20),
    )(value, *after)


def over_chips(mine):
    pieces = {0: mine}
    bit = 2
    while bit < lax.axis_size("obj"):
        for apart in sorted(pieces):
            pieces[apart ^ bit] = across(pieces[apart], bit)
        bit *= 2
    return pieces


def over_cores(pieces):
    if lax.axis_size("obj") > 1:
        for apart in sorted(pieces):
            pieces[apart ^ 1] = across(pieces[apart], 1)
    return [pieces[apart] for apart in range(len(pieces))]


def cost(micros):
    return pl.CostEstimate(flops=0, bytes_accessed=int(micros * 3_000_000), transcendentals=0)


def per_device(
    checkpoints,
    courant,
    insolation,
    region_mask,
    measure_step,
    snr_weight,
    diffusion_number,
    coupling,
    recombination,
):
    steps, fields, part = checkpoints.shape[:3]
    levels = snr_weight.shape[1]
    tiles = lax.axis_size("tile")
    parts = levels // part
    groups = fields // quads
    own = lanes // tiles
    halo = (window - own) // 2
    count = early_steps
    dims = (steps, groups, part, tiles, own, halo)
    spots = {"wind": count * groups * part}
    spots["cells"] = spots["wind"] + part
    rows = (up(spots["cells"] + 1, 8), up((steps - count) * groups * part, 8))
    short = levels // (tiles // quads)
    out_rows = up(groups * short + steps // 2 * fields, 8)
    limit = pltpu.CompilerParams(vmem_limit_bytes=24 * 2**20)
    in_vmem = pl.BlockSpec(memory_space=pltpu.VMEM)
    in_smem = pl.BlockSpec(memory_space=pltpu.SMEM)
    f32 = jnp.float32
    cell = (tiles, lanes)
    full = (levels * groups,) + cell

    packed = pl.pallas_call(
        functools.partial(pack_kernel, dims, rows, spots),
        out_shape=jax.ShapeDtypeStruct((tiles, sum(rows), lanes), jnp.bfloat16),
        in_specs=[pl.BlockSpec(memory_space=pltpu.HBM)] * 4,
        out_specs=in_vmem,
        scratch_shapes=[
            pltpu.VMEM((quads, sum(rows), lanes), f32),
            pltpu.VMEM((steps, fields, part, lanes), checkpoints.dtype),
            pltpu.VMEM((2, levels, lanes), f32),
            pltpu.VMEM((1, lanes), f32),
            pltpu.VMEM((1, lanes), jnp.int32),
            pltpu.SemaphoreType.DMA((4,)),
        ],
        compiler_params=pltpu.CompilerParams(vmem_limit_bytes=64 * 2**20),
        cost_estimate=cost(1),
    )(
        checkpoints.reshape(steps, fields, part, lanes),
        courant.reshape(2, levels, lanes),
        insolation,
        region_mask.reshape(1, lanes),
    )
    tables = pl.pallas_call(
        functools.partial(prepare_kernel, tiles),
        out_shape=(
            jax.ShapeDtypeStruct(full, f32),
            jax.ShapeDtypeStruct(((levels + 1) * groups,) + cell, f32),
            jax.ShapeDtypeStruct(full, f32),
            jax.ShapeDtypeStruct((groups * groups * quads,) + cell, f32),
            jax.ShapeDtypeStruct((groups,) + cell, f32),
        ),
        in_specs=[in_vmem] * 4,
        out_specs=(in_vmem,) * 5,
        scratch_shapes=[pltpu.VMEM((levels * 8, lanes), f32), pltpu.VMEM((levels * 8, lanes), f32)],
        compiler_params=limit,
        cost_estimate=cost(2),
    )(snr_weight, diffusion_number, coupling, recombination.reshape(fields, 1))

    strips = lax.all_to_all(packed, "tile", 0, 0, tiled=True)
    early = over_chips(strips[:, : rows[0]])
    late = over_chips(hold(strips[:, rows[0] :], *[early[apart] for apart in sorted(early)[1:]], tables[4]))
    early = over_cores(early)

    work = [pltpu.VMEM(full, f32), pltpu.VMEM((levels * groups * tiles, lanes), f32)]
    known = pl.pallas_call(
        functools.partial(early_kernel, dims, rows[0], spots, count, parts),
        out_shape=(
            jax.ShapeDtypeStruct((levels * groups, 2 * tiles, lanes), f32),
            jax.ShapeDtypeStruct((levels, 4) + cell, f32),
            jax.ShapeDtypeStruct((count * groups * levels, lanes), f32),
            jax.ShapeDtypeStruct((2,) + cell, f32),
        ),
        in_specs=[in_smem] + [in_vmem] * (parts + 5),
        out_specs=(in_vmem,) * 4,
        scratch_shapes=[pltpu.VMEM((parts * tiles * rows[0], lanes), f32)] + work,
        compiler_params=limit,
        cost_estimate=cost(5),
    )(measure_step, *early, *tables)

    late = over_cores({apart: hold(late[apart], known[3]) if apart else late[apart] for apart in late})
    result = pl.pallas_call(
        functools.partial(late_kernel, dims, rows[1], steps - count, parts, out_rows),
        out_shape=jax.ShapeDtypeStruct((tiles * out_rows, lanes), f32),
        in_specs=[in_smem] + [in_vmem] * (parts + 9),
        out_specs=in_vmem,
        scratch_shapes=[
            pltpu.VMEM((parts * tiles * rows[1], lanes), f32),
            pltpu.VMEM((levels * groups, 2 * tiles, lanes), f32),
            pltpu.VMEM(((steps - count) * groups * levels, lanes), f32),
        ]
        + work,
        compiler_params=limit,
        cost_estimate=cost(5),
    )(measure_step, *late, *tables, *known)
    home = lax.all_to_all(result.reshape(tiles, out_rows, lanes), "tile", 0, 0, tiled=True)

    state_adjoint, driver_grad = pl.pallas_call(
        functools.partial(unpack_kernel, (steps, groups, levels, fields, tiles, own, tiles * lanes)),
        out_shape=(
            jax.ShapeDtypeStruct((fields * levels, lanes), f32),
            jax.ShapeDtypeStruct((steps * fields, levels), f32),
        ),
        in_specs=[in_vmem],
        out_specs=(in_vmem, in_vmem),
        compiler_params=limit,
    )(home)
    return (state_adjoint.reshape(1, fields, levels, 1, lanes), driver_grad.reshape(1, steps, fields, levels))


def solution(mesh):
    return jax.shard_map(
        per_device,
        mesh=mesh,
        in_specs=(
            P(None, None, "obj", "tile", None),
            P(None, None, "tile", None),
            P("tile", None),
            P("obj", "tile", None),
            P("obj"),
            P(),
            P(),
            P(),
            P(),
        ),
        out_specs=(P("obj", None, None, "tile", None), P("obj", None, None, None)),
        check_vma=False,
    )
```

```python
import functools
import math

import jax
import jax.numpy as jnp
from jax import lax
from jax.experimental import pallas as pl
from jax.experimental.pallas import tpu as pltpu
from jax.sharding import PartitionSpec as P

smoothing = 0.2
lanes = 128
quads = 4
window = lanes // quads
exact = lax.Precision.HIGHEST
early_steps = 2
most = 32760.0
finest = 2.0**30
octave = 0.25 * math.log(2.0)


def up(value, unit):
    return -(-value // unit) * unit


def lane_iota(shape):
    return lax.broadcasted_iota(jnp.int32, shape, len(shape) - 1)


def pack_kernel(dims, rows, spots, *refs):
    outside, out, staged, inside, arrival = refs[:4], refs[4], refs[5], refs[6:10], refs[10]
    copies = [pltpu.make_async_copy(outside[i], inside[i], arrival.at[i]) for i in range(4)]
    for copy in copies:
        copy.start()
    for copy in copies:
        copy.wait()
    checkpoints, courant, insolation, region_mask = inside
    steps, groups, part, tiles, own, halo = dims
    count = early_steps
    ours = lax.axis_index("obj") * part
    total = sum(rows)
    for quad in range(quads):
        for back in range(steps):
            base = back * groups * part if back < count else rows[0] + (back - count) * groups * part
            for group in range(groups):
                at = base + group * part
                state = checkpoints[steps - 1 - back, group * quads + quad]
                staged[quad, at : at + part, :] = state.astype(jnp.float32)
    for way in range(2):
        wind = courant[way, pl.ds(ours, part), :]
        coarse = wind.astype(jnp.bfloat16).astype(jnp.float32)
        staged[2 * way, spots["wind"] : spots["wind"] + part, :] = coarse
        staged[2 * way + 1, spots["wind"] : spots["wind"] + part, :] = wind - coarse
    light = insolation[...]
    coarse = light.astype(jnp.bfloat16).astype(jnp.float32)
    middle = (light - coarse).astype(jnp.bfloat16).astype(jnp.float32)
    cells = [region_mask[...].astype(jnp.float32), coarse, middle, light - coarse - middle]
    ends = rows[0] + (steps - count) * groups * part
    for quad in range(quads):
        staged[quad, spots["cells"] : spots["cells"] + 1, :] = cells[quad]
        if spots["cells"] + 1 < rows[0]:
            rest = rows[0] - spots["cells"] - 1
            staged[quad, spots["cells"] + 1 : rows[0], :] = jnp.zeros((rest, lanes), jnp.float32)
        if ends < total:
            staged[quad, ends:total, :] = jnp.zeros((total - ends, lanes), jnp.float32)
    source = jnp.concatenate([staged[quad].astype(jnp.bfloat16) for quad in range(quads)], axis=1)
    for tile in range(tiles):
        shape = (quads * lanes, lanes)
        row = lax.broadcasted_iota(jnp.int32, shape, 0)
        lane = lane_iota(shape)
        wanted = (lane // window) * lanes + own * tile - halo + lane % window
        inside = own * tile - halo + lane % window
        pick = (row == wanted) & (inside >= 0) & (inside < lanes)
        pick = jnp.where(pick, 1.0, 0.0).astype(jnp.bfloat16)
        out[tile] = jnp.dot(source, pick, preferred_element_type=jnp.float32).astype(jnp.bfloat16)


def spread(values, group):
    fields = values.shape[0]
    shape = (fields, lanes)
    field = lax.broadcasted_iota(jnp.int32, shape, 0)
    chosen = jnp.where(field == group * quads + lane_iota(shape) // window, 1.0, 0.0)
    return lax.dot_general(
        values, chosen, (((0,), (0,)), ((), ())), precision=exact, preferred_element_type=jnp.float32
    )


def everywhere(quarter):
    quarter = jnp.where(lane_iota(quarter.shape) < window, quarter, 0.0)
    axis = len(quarter.shape) - 1
    quarter = quarter + pltpu.roll(quarter, window, axis)
    return quarter + pltpu.roll(quarter, 2 * window, axis)


def prepare_kernel(
    tiles, snr_weight, diffusion, coupling, recombination, snr, multiplier, inverse, mixing, loss, number, ratio
):
    fields, levels = snr_weight.shape
    groups = fields // quads
    cell = (tiles, lanes)
    for group in range(groups):
        spreaded = spread(snr_weight[...], group)
        for level in range(levels):
            snr[level * groups + group] = jnp.broadcast_to(spreaded[level : level + 1], cell)
        above = spread(diffusion[...], group)
        number[pl.ds(group, levels - 1, stride=8), :] = above
        number[pl.ds((levels - 1) * 8 + group, 1), :] = jnp.zeros((1, lanes), jnp.float32)

    valid = lax.broadcasted_iota(jnp.int32, (8, lanes), 0) < groups
    below = jnp.zeros((8, lanes), jnp.float32)
    last = jnp.ones((8, lanes), jnp.float32)
    earlier = jnp.zeros((8, lanes), jnp.float32)
    for level in range(levels):
        above = jnp.where(valid, number[level * 8 : level * 8 + 8, :], 0.0)
        now = (1.0 + below + above) * last - (below * below) * earlier
        turned = last / now
        ratio[level * 8 : level * 8 + 8, :] = turned
        number[level * 8 : level * 8 + 8, :] = above * turned
        earlier = last
        last = now
        below = above
    for group in range(groups):
        multiplier[group] = jnp.zeros(cell, jnp.float32)
        for level in range(levels):
            inverse[level * groups + group] = jnp.broadcast_to(ratio[level * 8 + group : level * 8 + group + 1, :], cell)
            multiplier[(level + 1) * groups + group] = jnp.broadcast_to(
                number[level * 8 + group : level * 8 + group + 1, :], cell
            )

    shape = (fields, fields)
    identity = jnp.where(lax.broadcasted_iota(jnp.int32, shape, 0) == lax.broadcasted_iota(jnp.int32, shape, 1), 1.0, 0.0)
    across = jnp.transpose(coupling[...] + identity)
    quarter = lane_iota((1, lanes)) // window
    for group in range(groups):
        columns = spread(across, group)
        for source in range(groups):
            for turn in range(quads):
                line = jnp.zeros((1, lanes), jnp.float32)
                for quad in range(quads):
                    field = source * quads + (quad - turn) % quads
                    line = jnp.where(quarter == quad, columns[field : field + 1], line)
                at = (group * groups + source) * quads + turn
                mixing[at] = jnp.broadcast_to(line, cell)
        loss[group] = jnp.broadcast_to(-2.0 * spread(recombination[...], group), cell)


def widen(dims, rows, pieces, wide):
    tiles = dims[3]
    me = lax.axis_index("obj")
    for apart, piece in enumerate(pieces):
        start = (me ^ apart) * (tiles * rows)
        for longitude in range(tiles):
            at = pl.multiple_of(start + longitude * rows, 8)
            wide[pl.ds(at, rows), :] = piece[longitude].astype(jnp.float32)


def steps_back(dims, rows, measure_step, first, count, mask, light, tables, wide, adjoint, coefs, sums, solving, lit):
    steps, groups, part, tiles, own, halo = dims
    snr, multiplier, inverse, mixing, loss = tables
    levels = adjoint.shape[0] // groups
    cell = (tiles, lanes)
    latitude = own * lax.axis_index("tile") - halo + lane_iota(cell) % window
    inside = jnp.where((latitude >= 0) & (latitude < lanes), 1.0, 0.0)
    centre = (1.0 - 4.0 * smoothing) * inside
    block = 12 if levels % 12 == 0 else levels
    together = 3 if block % 3 == 0 else 1
    nothing = tuple(jnp.zeros(cell, jnp.float32) for _ in range(groups))

    def step(back, carry):
        moment = first - back
        upcoming = jnp.where((measure_step[0] == moment) & (moment > 0), 1.0, 0.0)
        scored = upcoming * mask

        def forward(at, before):
            before = list(before)
            for inner in range(block):
                level = at * block + inner
                weight = [coefs[level, way] for way in range(4)]
                for group in range(groups):
                    row = level * groups + group
                    value = adjoint[row, 0:tiles]
                    moved = centre * value
                    moved = moved + weight[0] * adjoint[row, 1 : tiles + 1]
                    moved = moved + weight[1] * adjoint[row, tiles - 1 : 2 * tiles - 1]
                    moved = moved + weight[2] * pltpu.roll(value, lanes - 1, 1)
                    moved = moved + weight[3] * pltpu.roll(value, 1, 1)
                    moved = moved + multiplier[row] * before[group]
                    before[group] = moved
                    solving[row] = moved * inverse[row]
            return tuple(before)

        lax.fori_loop(0, levels // block, forward, nothing)

        def backward(at, after):
            after = list(after)
            for inner in range(0, block, together):
                pair = [levels - 1 - (at * block + inner + more) for more in range(together)]
                turned = []
                states = []
                for level in pair:
                    shifted = []
                    state = []
                    for group in range(groups):
                        row = level * groups + group
                        value = solving[row] + multiplier[row + groups] * after[group]
                        after[group] = value
                        lit[pl.ds(pl.multiple_of(row * tiles, 8), tiles), :] = value * light
                        shifted.append([value] + [pltpu.roll(value, window * turn, 1) for turn in range(1, quads)])
                        start = (level // part) * (tiles * rows) + (back * groups + group) * part + level % part
                        state.append(wide[pl.ds(start, tiles, stride=rows), :])
                    turned.append(shifted)
                    states.append(state)
                for group in range(groups):
                    result = [
                        loss[group] * states[at_pair][group] * turned[at_pair][group][0]
                        + scored * snr[pair[at_pair] * groups + group]
                        for at_pair in range(together)
                    ]
                    for source in range(groups):
                        for turn in range(quads):
                            factor = mixing[(group * groups + source) * quads + turn]
                            for at_pair in range(together):
                                result[at_pair] = result[at_pair] + factor * turned[at_pair][source][turn]
                    for at_pair in range(together):
                        row = pair[at_pair] * groups + group
                        adjoint[row, 0:tiles] = result[at_pair]
                        adjoint[row, tiles : 2 * tiles] = result[at_pair]
            return tuple(after)

        lax.fori_loop(0, levels // block, backward, nothing)
        for eight in range(levels * groups // 8):
            total = lit[pl.ds(eight * 8 * tiles, 8, stride=tiles), :]
            for longitude in range(1, tiles):
                total = total + lit[pl.ds(eight * 8 * tiles + longitude, 8, stride=tiles), :]
            sums[pl.ds(pl.multiple_of(back * (levels * groups) + eight * 8, 8), 8), :] = total
        return carry

    lax.fori_loop(0, count, step, 0)


def early_kernel(dims, rows, spots, count, parts, measure_step, *refs):
    pieces, refs = refs[:parts], refs[parts:]
    tables, refs = refs[:5], refs[5:]
    adjoint, coefs, sums, cells, wide, solving, lit = refs
    steps, groups, part, tiles, own, halo = dims
    levels = adjoint.shape[0] // groups
    widen(dims, rows, pieces, wide)
    cell = (tiles, lanes)
    spot = lane_iota(cell) % window
    latitude = own * lax.axis_index("tile") - halo + spot
    inside = jnp.where((latitude >= 0) & (latitude < lanes), 1.0, 0.0)

    def stored(piece, row):
        return wide[pl.ds(piece * (tiles * rows) + row, tiles, stride=rows), :]

    misc = stored(lax.axis_index("obj"), spots["cells"])
    mask = everywhere(misc)
    light = misc + pltpu.roll(misc, lanes - window, 1) + pltpu.roll(misc, lanes - 2 * window, 1)
    light = everywhere(pltpu.roll(light, lanes - window, 1))
    light = jnp.where((spot >= halo) & (spot < halo + own), light, 0.0)
    cells[0] = mask
    cells[1] = light

    for level in range(levels):
        both = stored(level // part, spots["wind"] + level % part)
        both = both + pltpu.roll(both, lanes - window, 1)
        east = everywhere(both)
        north = everywhere(pltpu.roll(both, lanes - 2 * window, 1))
        coefs[level, 0] = pltpu.roll(smoothing + 0.5 * east, tiles - 1, 0) * inside
        coefs[level, 1] = pltpu.roll(smoothing - 0.5 * east, 1, 0) * inside
        coefs[level, 2] = pltpu.roll(smoothing + 0.5 * north, lanes - 1, 1) * inside
        coefs[level, 3] = pltpu.roll(smoothing - 0.5 * north, 1, 1) * inside

    scored = jnp.where(measure_step[0] == steps, 1.0, 0.0) * mask
    for row in range(levels * groups):
        begin = scored * tables[0][row]
        adjoint[row, 0:tiles] = begin
        adjoint[row, tiles : 2 * tiles] = begin
    steps_back(
        dims, rows, measure_step, steps - 1, count, mask, light, tables, wide, adjoint, coefs, sums, solving, lit
    )


def late_kernel(dims, rows, count, parts, out_rows, measure_step, *refs):
    pieces, refs = refs[:parts], refs[parts:]
    tables, refs = refs[:5], refs[5:]
    given, coefs, early_sums, cells, out, wide, adjoint, sums, solving, lit, sent = refs
    steps, groups, part, tiles, own, halo = dims
    levels = adjoint.shape[0] // groups
    fields = groups * quads
    cell = (tiles, lanes)
    widen(dims, rows, pieces, wide)
    adjoint[...] = given[...]
    steps_back(
        dims,
        rows,
        measure_step,
        count - 1,
        count,
        cells[0],
        cells[1],
        tables,
        wide,
        adjoint,
        coefs,
        sums,
        solving,
        lit,
    )

    stack = tiles // quads
    short = levels // stack
    home = (lane_iota(cell) % window) // own
    largest = jnp.zeros(cell, jnp.float32)
    for group in range(groups):
        for level in range(short):
            whole = jnp.zeros(cell, jnp.float32)
            for high in range(stack):
                value = adjoint[(high * short + level) * groups + group, 0:tiles]
                turned = pltpu.roll(value, (high * own - halo) % lanes, 1)
                whole = jnp.where(home == high, turned, whole)
            largest = jnp.maximum(largest, jnp.abs(whole))
            sent[pl.ds(group * short + level, tiles, stride=out_rows), :] = whole
    power = exponent(largest)
    factor = jnp.exp(-octave * power) * most
    base = groups * short

    shape = (8, lanes)
    chosen = jnp.where(lax.broadcasted_iota(jnp.int32, shape, 0) == lane_iota(shape) // window, 1.0, 0.0)
    early = steps - count
    lines = []
    for back in range(steps):
        table, place = (early_sums, back) if back < early else (sums, back - early)
        for group in range(groups):
            lines.append(table[pl.ds(place * levels * groups + group, levels, stride=groups), :])
    width = up(steps * groups * levels, lanes)
    slack = width - steps * groups * levels
    total = lax.dot_general(
        chosen,
        jnp.concatenate(lines + [jnp.zeros((slack, lanes), jnp.float32)], axis=0),
        (((1,), (1,)), ((), ())),
        precision=exact,
        preferred_element_type=jnp.float32,
    )
    peak = exponent(jnp.max(jnp.abs(total), axis=(0, 1), keepdims=True))
    fixed = jnp.round(total * (jnp.exp(-octave * peak) * finest))
    coarse = jnp.floor(fixed * (1.0 / 65536.0) + 0.5)
    rest = fixed - coarse * 65536.0
    tall = width // lanes
    free = lane_iota((quads, lanes)) >= lanes - slack
    for longitude in range(tiles):
        at = longitude * out_rows
        sent[at : at + base, :] = jnp.round(sent[at : at + base, :] * factor[longitude : longitude + 1])
        line = power[longitude : longitude + 1]
        shown = jnp.concatenate([pltpu.roll(line, (lanes - window * (quad + 1)) % lanes, 1) for quad in range(quads)], axis=0)
        for tall_at in range(tall):
            high = coarse[:quads, tall_at * lanes : (tall_at + 1) * lanes]
            low = rest[:quads, tall_at * lanes : (tall_at + 1) * lanes]
            if tall_at == tall - 1:
                high = jnp.where(free, shown, high)
                low = jnp.where(free, peak, low)
            place = at + base + tall_at * quads
            sent[place : place + quads, :] = high
            sent[place + tall * quads : place + (tall + 1) * quads, :] = low
        used = base + 2 * tall * quads
        if used < out_rows:
            sent[at + used : at + out_rows, :] = jnp.zeros((out_rows - used, lanes), jnp.float32)
        out[longitude] = sent[at : at + out_rows, :].astype(jnp.int32).astype(jnp.int16)


def exponent(largest):
    return jnp.ceil(jnp.log(jnp.maximum(largest, 1e-30)) * (1.0 / octave) + 0.01)


def unpack_kernel(dims, arrived, state_adjoint, driver_grad):
    steps, groups, levels, fields, tiles, own, cells = dims
    stack = tiles // quads
    short = levels // stack
    base = groups * short
    width = up(steps * groups * levels, lanes)
    slack = width - steps * groups * levels
    tall = width // lanes
    quarter = lane_iota((1, lanes)) // window
    values = []
    total = jnp.zeros((tall * quads, lanes), jnp.float32)
    for tile in range(tiles):
        whole = arrived[tile].astype(jnp.int32).astype(jnp.float32)
        coarse = whole[base : base + tall * quads]
        rest = whole[base + tall * quads : base + 2 * tall * quads]
        power = jnp.zeros((1, lanes), jnp.float32)
        for quad in range(quads):
            line = coarse[(tall - 1) * quads + quad : (tall - 1) * quads + quad + 1]
            power = jnp.where(quarter == quad, pltpu.roll(line, window * (quad + 1) % lanes, 1), power)
        values.append(whole[0:base] * (jnp.exp(octave * power) * (1.0 / most)))
        peak = rest[(tall - 1) * quads : (tall - 1) * quads + 1, lanes - 1 : lanes]
        total = total + (coarse * 65536.0 + rest) * (jnp.exp(octave * peak) * (1.0 / finest))
    home = lane_iota((base, lanes)) // own
    apart = 1
    while apart < tiles:
        for low in range(tiles):
            if low & apart:
                continue
            first, second = values[low], values[low + apart]
            here = (home & apart) == 0
            values[low] = jnp.where(here, first, pltpu.roll(second, apart * own, 1))
            values[low + apart] = jnp.where(here, pltpu.roll(first, lanes - apart * own, 1), second)
        apart *= 2
    for high in range(stack):
        for quad in range(quads):
            for group in range(groups):
                at = (group * quads + quad) * levels + high * short
                state_adjoint[at : at + short, :] = values[quad * stack + high][group * short : (group + 1) * short]
    total = total / cells
    total = jnp.concatenate([total[at * quads : (at + 1) * quads] for at in range(tall)], axis=1)
    for back in range(steps):
        for group in range(groups):
            at = (steps - 1 - back) * fields + group * quads
            start = (back * groups + group) * levels
            driver_grad[at : at + quads, :] = total[:, start : start + levels]


def across(value, bit):
    count = lax.axis_size("obj")
    return lax.ppermute(value, "obj", [(place, place ^ bit) for place in range(count)])


def hold(value, *after):
    def copy(source, *refs):
        refs[-1][...] = source[...]

    near = pl.BlockSpec(memory_space=pltpu.VMEM)
    return pl.pallas_call(
        copy,
        out_shape=jax.ShapeDtypeStruct(value.shape, value.dtype),
        in_specs=[near] + [pl.BlockSpec(memory_space=pl.ANY)] * len(after),
        out_specs=near,
        compiler_params=pltpu.CompilerParams(vmem_limit_bytes=2 * 2**20),
    )(value, *after)


def over_chips(mine):
    pieces = {0: mine}
    bit = 2
    while bit < lax.axis_size("obj"):
        for apart in sorted(pieces):
            pieces[apart ^ bit] = across(pieces[apart], bit)
        bit *= 2
    return pieces


def over_cores(pieces):
    if lax.axis_size("obj") > 1:
        for apart in sorted(pieces):
            pieces[apart ^ 1] = across(pieces[apart], 1)
    return [pieces[apart] for apart in range(len(pieces))]


def cost(micros):
    return pl.CostEstimate(flops=0, bytes_accessed=int(micros * 3_000_000), transcendentals=0)


def per_device(
    checkpoints,
    courant,
    insolation,
    region_mask,
    measure_step,
    snr_weight,
    diffusion_number,
    coupling,
    recombination,
):
    steps, fields, part = checkpoints.shape[:3]
    levels = snr_weight.shape[1]
    tiles = lax.axis_size("tile")
    parts = levels // part
    groups = fields // quads
    own = lanes // tiles
    halo = (window - own) // 2
    count = early_steps
    dims = (steps, groups, part, tiles, own, halo)
    spots = {"wind": count * groups * part}
    spots["cells"] = spots["wind"] + part
    rows = (up(spots["cells"] + 1, 8), up((steps - count) * groups * part, 8))
    short = levels // (tiles // quads)
    out_rows = up(groups * short + 2 * quads * up(steps * groups * levels, lanes) // lanes, 16)
    limit = pltpu.CompilerParams(vmem_limit_bytes=24 * 2**20)
    in_vmem = pl.BlockSpec(memory_space=pltpu.VMEM)
    in_smem = pl.BlockSpec(memory_space=pltpu.SMEM)
    f32 = jnp.float32
    cell = (tiles, lanes)
    full = (levels * groups,) + cell

    packed = pl.pallas_call(
        functools.partial(pack_kernel, dims, rows, spots),
        out_shape=jax.ShapeDtypeStruct((tiles, sum(rows), lanes), jnp.bfloat16),
        in_specs=[pl.BlockSpec(memory_space=pltpu.HBM)] * 4,
        out_specs=in_vmem,
        scratch_shapes=[
            pltpu.VMEM((quads, sum(rows), lanes), f32),
            pltpu.VMEM((steps, fields, part, lanes), checkpoints.dtype),
            pltpu.VMEM((2, levels, lanes), f32),
            pltpu.VMEM((1, lanes), f32),
            pltpu.VMEM((1, lanes), jnp.int32),
            pltpu.SemaphoreType.DMA((4,)),
        ],
        compiler_params=pltpu.CompilerParams(vmem_limit_bytes=64 * 2**20),
        cost_estimate=cost(1),
    )(
        checkpoints.reshape(steps, fields, part, lanes),
        courant.reshape(2, levels, lanes),
        insolation,
        region_mask.reshape(1, lanes),
    )
    tables = pl.pallas_call(
        functools.partial(prepare_kernel, tiles),
        out_shape=(
            jax.ShapeDtypeStruct(full, f32),
            jax.ShapeDtypeStruct(((levels + 1) * groups,) + cell, f32),
            jax.ShapeDtypeStruct(full, f32),
            jax.ShapeDtypeStruct((groups * groups * quads,) + cell, f32),
            jax.ShapeDtypeStruct((groups,) + cell, f32),
        ),
        in_specs=[in_vmem] * 4,
        out_specs=(in_vmem,) * 5,
        scratch_shapes=[pltpu.VMEM((levels * 8, lanes), f32), pltpu.VMEM((levels * 8, lanes), f32)],
        compiler_params=limit,
        cost_estimate=cost(2),
    )(snr_weight, diffusion_number, coupling, recombination.reshape(fields, 1))

    strips = lax.all_to_all(packed, "tile", 0, 0, tiled=True)
    early = over_chips(strips[:, : rows[0]])
    late = over_chips(hold(strips[:, rows[0] :], *[early[apart] for apart in sorted(early)[1:]], tables[4]))
    early = over_cores(early)

    work = [pltpu.VMEM(full, f32), pltpu.VMEM((levels * groups * tiles, lanes), f32)]
    known = pl.pallas_call(
        functools.partial(early_kernel, dims, rows[0], spots, count, parts),
        out_shape=(
            jax.ShapeDtypeStruct((levels * groups, 2 * tiles, lanes), f32),
            jax.ShapeDtypeStruct((levels, 4) + cell, f32),
            jax.ShapeDtypeStruct((count * groups * levels, lanes), f32),
            jax.ShapeDtypeStruct((2,) + cell, f32),
        ),
        in_specs=[in_smem] + [in_vmem] * (parts + 5),
        out_specs=(in_vmem,) * 4,
        scratch_shapes=[pltpu.VMEM((parts * tiles * rows[0], lanes), f32)] + work,
        compiler_params=limit,
        cost_estimate=cost(5),
    )(measure_step, *early, *tables)

    late = over_cores({apart: hold(late[apart], known[3]) if apart else late[apart] for apart in late})
    result = pl.pallas_call(
        functools.partial(late_kernel, dims, rows[1], steps - count, parts, out_rows),
        out_shape=jax.ShapeDtypeStruct((tiles, out_rows, lanes), jnp.int16),
        in_specs=[in_smem] + [in_vmem] * (parts + 9),
        out_specs=in_vmem,
        scratch_shapes=[
            pltpu.VMEM((parts * tiles * rows[1], lanes), f32),
            pltpu.VMEM((levels * groups, 2 * tiles, lanes), f32),
            pltpu.VMEM(((steps - count) * groups * levels, lanes), f32),
        ]
        + work
        + [pltpu.VMEM((tiles * out_rows, lanes), f32)],
        compiler_params=limit,
        cost_estimate=cost(5),
    )(measure_step, *late, *tables, *known)
    home = lax.all_to_all(result, "tile", 0, 0, tiled=True)

    state_adjoint, driver_grad = pl.pallas_call(
        functools.partial(unpack_kernel, (steps, groups, levels, fields, tiles, own, tiles * lanes)),
        out_shape=(
            jax.ShapeDtypeStruct((fields * levels, lanes), f32),
            jax.ShapeDtypeStruct((steps * fields, levels), f32),
        ),
        in_specs=[in_vmem],
        out_specs=(in_vmem, in_vmem),
        compiler_params=limit,
    )(home)
    return (state_adjoint.reshape(1, fields, levels, 1, lanes), driver_grad.reshape(1, steps, fields, levels))


def solution(mesh):
    return jax.shard_map(
        per_device,
        mesh=mesh,
        in_specs=(
            P(None, None, "obj", "tile", None),
            P(None, None, "tile", None),
            P("tile", None),
            P("obj", "tile", None),
            P("obj"),
            P(),
            P(),
            P(),
            P(),
        ),
        out_specs=(P("obj", None, None, "tile", None), P("obj", None, None, None)),
        check_vma=False,
    )
```

```python
import functools
import math

import jax
import jax.numpy as jnp
from jax import lax
from jax.experimental import pallas as pl
from jax.experimental.pallas import tpu as pltpu
from jax.sharding import PartitionSpec as P

smoothing = 0.2
lanes = 128
quads = 4
window = lanes // quads
exact = lax.Precision.HIGHEST
early_steps = 3
most = 32760.0
finest = 2.0**30
octave = 0.25 * math.log(2.0)


def up(value, unit):
    return -(-value // unit) * unit


def lane_iota(shape):
    return lax.broadcasted_iota(jnp.int32, shape, len(shape) - 1)


def pack_kernel(dims, rows, spots, *refs):
    outside, first, second, staged, inside, arrival = refs[:4], refs[4], refs[5], refs[6], refs[7:11], refs[11]
    copies = [pltpu.make_async_copy(outside[i], inside[i], arrival.at[i]) for i in range(4)]
    for copy in copies:
        copy.start()
    for copy in copies:
        copy.wait()
    checkpoints, courant, insolation, region_mask = inside
    steps, groups, part, tiles, own, halo = dims
    count = early_steps
    ours = lax.axis_index("obj") * part
    total = sum(rows)
    for quad in range(quads):
        for back in range(steps):
            base = back * groups * part if back < count else rows[0] + (back - count) * groups * part
            for group in range(groups):
                at = base + group * part
                state = checkpoints[steps - 1 - back, group * quads + quad]
                staged[quad, at : at + part, :] = state.astype(jnp.float32)
    for way in range(2):
        wind = courant[way, pl.ds(ours, part), :]
        coarse = wind.astype(jnp.bfloat16).astype(jnp.float32)
        staged[2 * way, spots["wind"] : spots["wind"] + part, :] = coarse
        staged[2 * way + 1, spots["wind"] : spots["wind"] + part, :] = wind - coarse
    light = insolation[...]
    coarse = light.astype(jnp.bfloat16).astype(jnp.float32)
    middle = (light - coarse).astype(jnp.bfloat16).astype(jnp.float32)
    cells = [region_mask[...].astype(jnp.float32), coarse, middle, light - coarse - middle]
    ends = rows[0] + (steps - count) * groups * part
    for quad in range(quads):
        staged[quad, spots["cells"] : spots["cells"] + 1, :] = cells[quad]
        if spots["cells"] + 1 < rows[0]:
            rest = rows[0] - spots["cells"] - 1
            staged[quad, spots["cells"] + 1 : rows[0], :] = jnp.zeros((rest, lanes), jnp.float32)
        if ends < total:
            staged[quad, ends:total, :] = jnp.zeros((total - ends, lanes), jnp.float32)
    source = jnp.concatenate([staged[quad].astype(jnp.bfloat16) for quad in range(quads)], axis=1)
    for tile in range(tiles):
        shape = (quads * lanes, lanes)
        row = lax.broadcasted_iota(jnp.int32, shape, 0)
        lane = lane_iota(shape)
        wanted = (lane // window) * lanes + own * tile - halo + lane % window
        inside = own * tile - halo + lane % window
        pick = (row == wanted) & (inside >= 0) & (inside < lanes)
        pick = jnp.where(pick, 1.0, 0.0).astype(jnp.bfloat16)
        cut = jnp.dot(source, pick, preferred_element_type=jnp.float32).astype(jnp.bfloat16)
        first[tile] = cut[: rows[0]]
        second[tile] = cut[rows[0] :]


def spread(values, group):
    fields = values.shape[0]
    shape = (fields, lanes)
    field = lax.broadcasted_iota(jnp.int32, shape, 0)
    chosen = jnp.where(field == group * quads + lane_iota(shape) // window, 1.0, 0.0)
    return lax.dot_general(
        values, chosen, (((0,), (0,)), ((), ())), precision=exact, preferred_element_type=jnp.float32
    )


def everywhere(quarter):
    quarter = jnp.where(lane_iota(quarter.shape) < window, quarter, 0.0)
    axis = len(quarter.shape) - 1
    quarter = quarter + pltpu.roll(quarter, window, axis)
    return quarter + pltpu.roll(quarter, 2 * window, axis)


def prepare_kernel(
    tiles, snr_weight, diffusion, coupling, recombination, snr, multiplier, inverse, mixing, loss, number, ratio
):
    fields, levels = snr_weight.shape
    groups = fields // quads
    cell = (tiles, lanes)
    for group in range(groups):
        spreaded = spread(snr_weight[...], group)
        for level in range(levels):
            snr[level * groups + group] = jnp.broadcast_to(spreaded[level : level + 1], cell)
        above = spread(diffusion[...], group)
        number[pl.ds(group, levels - 1, stride=8), :] = above
        number[pl.ds((levels - 1) * 8 + group, 1), :] = jnp.zeros((1, lanes), jnp.float32)

    valid = lax.broadcasted_iota(jnp.int32, (8, lanes), 0) < groups
    below = jnp.zeros((8, lanes), jnp.float32)
    last = jnp.ones((8, lanes), jnp.float32)
    earlier = jnp.zeros((8, lanes), jnp.float32)
    for level in range(levels):
        above = jnp.where(valid, number[level * 8 : level * 8 + 8, :], 0.0)
        now = (1.0 + below + above) * last - (below * below) * earlier
        turned = last / now
        ratio[level * 8 : level * 8 + 8, :] = turned
        number[level * 8 : level * 8 + 8, :] = above * turned
        earlier = last
        last = now
        below = above
    for group in range(groups):
        multiplier[group] = jnp.zeros(cell, jnp.float32)
        for level in range(levels):
            inverse[level * groups + group] = jnp.broadcast_to(ratio[level * 8 + group : level * 8 + group + 1, :], cell)
            multiplier[(level + 1) * groups + group] = jnp.broadcast_to(
                number[level * 8 + group : level * 8 + group + 1, :], cell
            )

    shape = (fields, fields)
    identity = jnp.where(lax.broadcasted_iota(jnp.int32, shape, 0) == lax.broadcasted_iota(jnp.int32, shape, 1), 1.0, 0.0)
    across = jnp.transpose(coupling[...] + identity)
    quarter = lane_iota((1, lanes)) // window
    for group in range(groups):
        columns = spread(across, group)
        for source in range(groups):
            for turn in range(quads):
                line = jnp.zeros((1, lanes), jnp.float32)
                for quad in range(quads):
                    field = source * quads + (quad - turn) % quads
                    line = jnp.where(quarter == quad, columns[field : field + 1], line)
                at = (group * groups + source) * quads + turn
                mixing[at] = jnp.broadcast_to(line, cell)
        loss[group] = jnp.broadcast_to(-2.0 * spread(recombination[...], group), cell)


def widen(dims, rows, pieces, wide):
    tiles = dims[3]
    me = lax.axis_index("obj")
    for apart, piece in enumerate(pieces):
        start = (me ^ apart) * (tiles * rows)
        for longitude in range(tiles):
            at = pl.multiple_of(start + longitude * rows, 8)
            wide[pl.ds(at, rows), :] = piece[longitude].astype(jnp.float32)


def steps_back(dims, rows, measure_step, first, count, mask, light, tables, wide, adjoint, coefs, sums, solving, lit):
    steps, groups, part, tiles, own, halo = dims
    snr, multiplier, inverse, mixing, loss = tables
    levels = adjoint.shape[0] // groups
    cell = (tiles, lanes)
    latitude = own * lax.axis_index("tile") - halo + lane_iota(cell) % window
    inside = jnp.where((latitude >= 0) & (latitude < lanes), 1.0, 0.0)
    centre = (1.0 - 4.0 * smoothing) * inside
    block = levels
    together = 3 if block % 3 == 0 else 1
    nothing = tuple(jnp.zeros(cell, jnp.float32) for _ in range(groups))

    def step(back, carry):
        moment = first - back
        scored = jnp.where((measure_step[...] == moment) & (moment > 0), 1.0, 0.0) * mask

        def forward(at, before):
            before = list(before)
            for inner in range(block):
                level = at * block + inner
                weight = [coefs[level, way] for way in range(4)]
                for group in range(groups):
                    row = level * groups + group
                    value = adjoint[row, 0:tiles]
                    moved = centre * value
                    moved = moved + weight[0] * adjoint[row, 1 : tiles + 1]
                    moved = moved + weight[1] * adjoint[row, tiles - 1 : 2 * tiles - 1]
                    moved = moved + weight[2] * pltpu.roll(value, lanes - 1, 1)
                    moved = moved + weight[3] * pltpu.roll(value, 1, 1)
                    moved = moved + multiplier[row] * before[group]
                    before[group] = moved
                    solving[row] = moved * inverse[row]
            return tuple(before)

        lax.fori_loop(0, levels // block, forward, nothing)

        def backward(at, after):
            after = list(after)
            for inner in range(0, block, together):
                pair = [levels - 1 - (at * block + inner + more) for more in range(together)]
                turned = []
                states = []
                for level in pair:
                    shifted = []
                    state = []
                    for group in range(groups):
                        row = level * groups + group
                        value = solving[row] + multiplier[row + groups] * after[group]
                        after[group] = value
                        lit[pl.ds(pl.multiple_of(row * tiles, 8), tiles), :] = value * light
                        shifted.append([value] + [pltpu.roll(value, window * turn, 1) for turn in range(1, quads)])
                        start = (level // part) * (tiles * rows) + (back * groups + group) * part + level % part
                        state.append(wide[pl.ds(start, tiles, stride=rows), :])
                    turned.append(shifted)
                    states.append(state)
                for group in range(groups):
                    result = [
                        loss[group] * states[at_pair][group] * turned[at_pair][group][0]
                        + scored * snr[pair[at_pair] * groups + group]
                        for at_pair in range(together)
                    ]
                    for source in range(groups):
                        for turn in range(quads):
                            factor = mixing[(group * groups + source) * quads + turn]
                            for at_pair in range(together):
                                result[at_pair] = result[at_pair] + factor * turned[at_pair][source][turn]
                    for at_pair in range(together):
                        row = pair[at_pair] * groups + group
                        adjoint[row, 0:tiles] = result[at_pair]
                        adjoint[row, tiles : 2 * tiles] = result[at_pair]
            return tuple(after)

        lax.fori_loop(0, levels // block, backward, nothing)
        for eight in range(levels * groups // 8):
            total = lit[pl.ds(eight * 8 * tiles, 8, stride=tiles), :]
            for longitude in range(1, tiles):
                total = total + lit[pl.ds(eight * 8 * tiles + longitude, 8, stride=tiles), :]
            sums[pl.ds(pl.multiple_of(back * (levels * groups) + eight * 8, 8), 8), :] = total
        return carry

    lax.fori_loop(0, count, step, 0)


def early_kernel(dims, rows, spots, count, parts, measure_step, *refs):
    pieces, refs = refs[:parts], refs[parts:]
    tables, refs = refs[:5], refs[5:]
    adjoint, coefs, sums, cells, wide, solving, lit = refs
    steps, groups, part, tiles, own, halo = dims
    levels = adjoint.shape[0] // groups
    widen(dims, rows, pieces, wide)
    cell = (tiles, lanes)
    spot = lane_iota(cell) % window
    latitude = own * lax.axis_index("tile") - halo + spot
    inside = jnp.where((latitude >= 0) & (latitude < lanes), 1.0, 0.0)

    def stored(piece, row):
        return wide[pl.ds(piece * (tiles * rows) + row, tiles, stride=rows), :]

    misc = stored(lax.axis_index("obj"), spots["cells"])
    mask = everywhere(misc)
    light = misc + pltpu.roll(misc, lanes - window, 1) + pltpu.roll(misc, lanes - 2 * window, 1)
    light = everywhere(pltpu.roll(light, lanes - window, 1))
    light = jnp.where((spot >= halo) & (spot < halo + own), light, 0.0)
    cells[0] = mask
    cells[1] = light

    for level in range(levels):
        both = stored(level // part, spots["wind"] + level % part)
        both = both + pltpu.roll(both, lanes - window, 1)
        east = everywhere(both)
        north = everywhere(pltpu.roll(both, lanes - 2 * window, 1))
        coefs[level, 0] = pltpu.roll(smoothing + 0.5 * east, tiles - 1, 0) * inside
        coefs[level, 1] = pltpu.roll(smoothing - 0.5 * east, 1, 0) * inside
        coefs[level, 2] = pltpu.roll(smoothing + 0.5 * north, lanes - 1, 1) * inside
        coefs[level, 3] = pltpu.roll(smoothing - 0.5 * north, 1, 1) * inside

    scored = jnp.where(measure_step[...] == steps, 1.0, 0.0) * mask
    for row in range(levels * groups):
        begin = scored * tables[0][row]
        adjoint[row, 0:tiles] = begin
        adjoint[row, tiles : 2 * tiles] = begin
    steps_back(
        dims, rows, measure_step, steps - 1, count, mask, light, tables, wide, adjoint, coefs, sums, solving, lit
    )


def late_kernel(dims, rows, count, parts, out_rows, measure_step, *refs):
    pieces, refs = refs[:parts], refs[parts:]
    tables, refs = refs[:5], refs[5:]
    given, coefs, early_sums, cells, out, wide, adjoint, sums, solving, lit, sent = refs
    steps, groups, part, tiles, own, halo = dims
    levels = adjoint.shape[0] // groups
    fields = groups * quads
    cell = (tiles, lanes)
    widen(dims, rows, pieces, wide)
    adjoint[...] = given[...]
    steps_back(
        dims,
        rows,
        measure_step,
        count - 1,
        count,
        cells[0],
        cells[1],
        tables,
        wide,
        adjoint,
        coefs,
        sums,
        solving,
        lit,
    )

    stack = tiles // quads
    short = levels // stack
    home = (lane_iota(cell) % window) // own
    largest = jnp.zeros(cell, jnp.float32)
    for group in range(groups):
        for level in range(short):
            whole = jnp.zeros(cell, jnp.float32)
            for high in range(stack):
                value = adjoint[(high * short + level) * groups + group, 0:tiles]
                turned = pltpu.roll(value, (high * own - halo) % lanes, 1)
                whole = jnp.where(home == high, turned, whole)
            largest = jnp.maximum(largest, jnp.abs(whole))
            sent[pl.ds(group * short + level, tiles, stride=out_rows), :] = whole
    power = exponent(largest)
    factor = jnp.exp(-octave * power) * most
    base = groups * short

    shape = (8, lanes)
    chosen = jnp.where(lax.broadcasted_iota(jnp.int32, shape, 0) == lane_iota(shape) // window, 1.0, 0.0)
    early = steps - count
    lines = []
    for back in range(steps):
        table, place = (early_sums, back) if back < early else (sums, back - early)
        for group in range(groups):
            lines.append(table[pl.ds(place * levels * groups + group, levels, stride=groups), :])
    width = up(steps * groups * levels, lanes)
    slack = width - steps * groups * levels
    total = lax.dot_general(
        chosen,
        jnp.concatenate(lines + [jnp.zeros((slack, lanes), jnp.float32)], axis=0),
        (((1,), (1,)), ((), ())),
        precision=exact,
        preferred_element_type=jnp.float32,
    )
    peak = exponent(jnp.max(jnp.abs(total), axis=(0, 1), keepdims=True))
    fixed = jnp.round(total * (jnp.exp(-octave * peak) * finest))
    coarse = jnp.floor(fixed * (1.0 / 65536.0) + 0.5)
    rest = fixed - coarse * 65536.0
    tall = width // lanes
    free = lane_iota((quads, lanes)) >= lanes - slack
    for longitude in range(tiles):
        at = longitude * out_rows
        sent[at : at + base, :] = jnp.round(sent[at : at + base, :] * factor[longitude : longitude + 1])
        line = power[longitude : longitude + 1]
        shown = jnp.concatenate([pltpu.roll(line, (lanes - window * (quad + 1)) % lanes, 1) for quad in range(quads)], axis=0)
        for tall_at in range(tall):
            high = coarse[:quads, tall_at * lanes : (tall_at + 1) * lanes]
            low = rest[:quads, tall_at * lanes : (tall_at + 1) * lanes]
            if tall_at == tall - 1:
                high = jnp.where(free, shown, high)
                low = jnp.where(free, peak, low)
            place = at + base + tall_at * quads
            sent[place : place + quads, :] = high
            sent[place + tall * quads : place + (tall + 1) * quads, :] = low
        used = base + 2 * tall * quads
        if used < out_rows:
            sent[at + used : at + out_rows, :] = jnp.zeros((out_rows - used, lanes), jnp.float32)
        out[longitude] = sent[at : at + out_rows, :].astype(jnp.int32).astype(jnp.int16)


def exponent(largest):
    return jnp.ceil(jnp.log(jnp.maximum(largest, 1e-30)) * (1.0 / octave) + 0.01)


def unpack_kernel(dims, arrived, state_adjoint, driver_grad):
    steps, groups, levels, fields, tiles, own, cells = dims
    stack = tiles // quads
    short = levels // stack
    base = groups * short
    width = up(steps * groups * levels, lanes)
    slack = width - steps * groups * levels
    tall = width // lanes
    quarter = lane_iota((1, lanes)) // window
    values = []
    total = jnp.zeros((tall * quads, lanes), jnp.float32)
    for tile in range(tiles):
        whole = arrived[tile].astype(jnp.int32).astype(jnp.float32)
        coarse = whole[base : base + tall * quads]
        rest = whole[base + tall * quads : base + 2 * tall * quads]
        power = jnp.zeros((1, lanes), jnp.float32)
        for quad in range(quads):
            line = coarse[(tall - 1) * quads + quad : (tall - 1) * quads + quad + 1]
            power = jnp.where(quarter == quad, pltpu.roll(line, window * (quad + 1) % lanes, 1), power)
        values.append(whole[0:base] * (jnp.exp(octave * power) * (1.0 / most)))
        peak = rest[(tall - 1) * quads : (tall - 1) * quads + 1, lanes - 1 : lanes]
        total = total + (coarse * 65536.0 + rest) * (jnp.exp(octave * peak) * (1.0 / finest))
    home = lane_iota((base, lanes)) // own
    apart = 1
    while apart < tiles:
        for low in range(tiles):
            if low & apart:
                continue
            first, second = values[low], values[low + apart]
            here = (home & apart) == 0
            values[low] = jnp.where(here, first, pltpu.roll(second, apart * own, 1))
            values[low + apart] = jnp.where(here, pltpu.roll(first, lanes - apart * own, 1), second)
        apart *= 2
    for high in range(stack):
        for quad in range(quads):
            for group in range(groups):
                at = (group * quads + quad) * levels + high * short
                state_adjoint[at : at + short, :] = values[quad * stack + high][group * short : (group + 1) * short]
    total = total / cells
    total = jnp.concatenate([total[at * quads : (at + 1) * quads] for at in range(tall)], axis=1)
    for back in range(steps):
        for group in range(groups):
            at = (steps - 1 - back) * fields + group * quads
            start = (back * groups + group) * levels
            driver_grad[at : at + quads, :] = total[:, start : start + levels]


def across(value, bit):
    count = lax.axis_size("obj")
    return lax.ppermute(value, "obj", [(place, place ^ bit) for place in range(count)])


def hold(value, *after):
    def copy(source, *refs):
        refs[-1][...] = source[...]

    near = pl.BlockSpec(memory_space=pltpu.VMEM)
    return pl.pallas_call(
        copy,
        out_shape=jax.ShapeDtypeStruct(value.shape, value.dtype),
        in_specs=[near] + [pl.BlockSpec(memory_space=pl.ANY)] * len(after),
        out_specs=near,
        compiler_params=pltpu.CompilerParams(vmem_limit_bytes=2 * 2**20),
    )(value, *after)


def over_chips(mine):
    pieces = {0: mine}
    bit = 2
    while bit < lax.axis_size("obj"):
        for apart in sorted(pieces):
            pieces[apart ^ bit] = across(pieces[apart], bit)
        bit *= 2
    return pieces


def over_cores(pieces):
    if lax.axis_size("obj") > 1:
        for apart in sorted(pieces):
            pieces[apart ^ 1] = across(pieces[apart], 1)
    return [pieces[apart] for apart in range(len(pieces))]


def cost(micros):
    return pl.CostEstimate(flops=0, bytes_accessed=int(micros * 3_000_000), transcendentals=0)


def per_device(
    checkpoints,
    courant,
    insolation,
    region_mask,
    measure_step,
    snr_weight,
    diffusion_number,
    coupling,
    recombination,
):
    steps, fields, part = checkpoints.shape[:3]
    levels = snr_weight.shape[1]
    tiles = lax.axis_size("tile")
    parts = levels // part
    groups = fields // quads
    own = lanes // tiles
    halo = (window - own) // 2
    count = early_steps
    dims = (steps, groups, part, tiles, own, halo)
    spots = {"wind": count * groups * part}
    spots["cells"] = spots["wind"] + part
    rows = (up(spots["cells"] + 1, 16), up((steps - count) * groups * part, 16))
    short = levels // (tiles // quads)
    out_rows = up(groups * short + 2 * quads * up(steps * groups * levels, lanes) // lanes, 16)
    limit = pltpu.CompilerParams(vmem_limit_bytes=24 * 2**20)
    in_vmem = pl.BlockSpec(memory_space=pltpu.VMEM)
    f32 = jnp.float32
    cell = (tiles, lanes)
    full = (levels * groups,) + cell

    packed, packed_late = pl.pallas_call(
        functools.partial(pack_kernel, dims, rows, spots),
        out_shape=tuple(jax.ShapeDtypeStruct((tiles, size, lanes), jnp.bfloat16) for size in rows),
        in_specs=[pl.BlockSpec(memory_space=pltpu.HBM)] * 4,
        out_specs=(in_vmem, in_vmem),
        scratch_shapes=[
            pltpu.VMEM((quads, sum(rows), lanes), f32),
            pltpu.VMEM((steps, fields, part, lanes), checkpoints.dtype),
            pltpu.VMEM((2, levels, lanes), f32),
            pltpu.VMEM((1, lanes), f32),
            pltpu.VMEM((1, lanes), jnp.int32),
            pltpu.SemaphoreType.DMA((4,)),
        ],
        compiler_params=pltpu.CompilerParams(vmem_limit_bytes=64 * 2**20),
        cost_estimate=cost(1),
    )(
        checkpoints.reshape(steps, fields, part, lanes),
        courant.reshape(2, levels, lanes),
        insolation,
        region_mask.reshape(1, lanes),
    )
    tables = pl.pallas_call(
        functools.partial(prepare_kernel, tiles),
        out_shape=(
            jax.ShapeDtypeStruct(full, f32),
            jax.ShapeDtypeStruct(((levels + 1) * groups,) + cell, f32),
            jax.ShapeDtypeStruct(full, f32),
            jax.ShapeDtypeStruct((groups * groups * quads,) + cell, f32),
            jax.ShapeDtypeStruct((groups,) + cell, f32),
        ),
        in_specs=[in_vmem] * 4,
        out_specs=(in_vmem,) * 5,
        scratch_shapes=[pltpu.VMEM((levels * 8, lanes), f32), pltpu.VMEM((levels * 8, lanes), f32)],
        compiler_params=limit,
        cost_estimate=cost(2),
    )(snr_weight, diffusion_number, coupling, recombination.reshape(fields, 1))

    strips = lax.all_to_all(packed, "tile", 0, 0, tiled=True)
    early = over_chips(strips)
    strips_late = lax.all_to_all(hold(packed_late, strips), "tile", 0, 0, tiled=True)
    early = over_cores({apart: hold(early[apart], strips_late) if apart else early[apart] for apart in early})
    late = over_chips(strips_late)

    work = [pltpu.VMEM(full, f32), pltpu.VMEM((levels * groups * tiles, lanes), f32)]
    known = pl.pallas_call(
        functools.partial(early_kernel, dims, rows[0], spots, count, parts),
        out_shape=(
            jax.ShapeDtypeStruct((levels * groups, 2 * tiles, lanes), f32),
            jax.ShapeDtypeStruct((levels, 4) + cell, f32),
            jax.ShapeDtypeStruct((count * groups * levels, lanes), f32),
            jax.ShapeDtypeStruct((2,) + cell, f32),
        ),
        in_specs=[in_vmem] * (1 + parts + 5),
        out_specs=(in_vmem,) * 4,
        scratch_shapes=[pltpu.VMEM((parts * tiles * rows[0], lanes), f32)] + work,
        compiler_params=limit,
        cost_estimate=cost(5),
    )(measure_step.reshape(1, 1), *early, *tables)

    late = over_cores({apart: hold(late[apart], known[3]) if apart else late[apart] for apart in late})
    result = pl.pallas_call(
        functools.partial(late_kernel, dims, rows[1], steps - count, parts, out_rows),
        out_shape=jax.ShapeDtypeStruct((tiles, out_rows, lanes), jnp.int16),
        in_specs=[in_vmem] * (1 + parts + 9),
        out_specs=in_vmem,
        scratch_shapes=[
            pltpu.VMEM((parts * tiles * rows[1], lanes), f32),
            pltpu.VMEM((levels * groups, 2 * tiles, lanes), f32),
            pltpu.VMEM(((steps - count) * groups * levels, lanes), f32),
        ]
        + work
        + [pltpu.VMEM((tiles * out_rows, lanes), f32)],
        compiler_params=limit,
        cost_estimate=cost(5),
    )(measure_step.reshape(1, 1), *late, *tables, *known)
    home = lax.all_to_all(result, "tile", 0, 0, tiled=True)

    state_adjoint, driver_grad = pl.pallas_call(
        functools.partial(unpack_kernel, (steps, groups, levels, fields, tiles, own, tiles * lanes)),
        out_shape=(
            jax.ShapeDtypeStruct((fields * levels, lanes), f32),
            jax.ShapeDtypeStruct((steps * fields, levels), f32),
        ),
        in_specs=[in_vmem],
        out_specs=(in_vmem, in_vmem),
        compiler_params=limit,
    )(home)
    return (state_adjoint.reshape(1, fields, levels, 1, lanes), driver_grad.reshape(1, steps, fields, levels))


def solution(mesh):
    return jax.shard_map(
        per_device,
        mesh=mesh,
        in_specs=(
            P(None, None, "obj", "tile", None),
            P(None, None, "tile", None),
            P("tile", None),
            P("obj", "tile", None),
            P("obj"),
            P(),
            P(),
            P(),
            P(),
        ),
        out_specs=(P("obj", None, None, "tile", None), P("obj", None, None, None)),
        check_vma=False,
    )
```
